32 devices in a mesh: group: 2 (over x), inp: 8 (over z, y), out: 2 (over core).
Axes of the slice: x: 2, y: 2, z: 4, core: 2. Of those that a mesh axis runs over, the one named last changes fastest.
Arguments:
- acts: bfloat16 [4, 512, 28672], P(('group', 'out'), None, 'inp'), parts along dimension 0, may hold values from -6 to 6
- grads: bfloat16 [4, 512, 8192], P(('group', 'out'), None, 'inp'), parts along dimension 0, may hold values from -6 to 6
- basis_a: bfloat16 [57344, 4096], P(('group', 'inp')), parts along dimension 0, may hold values from -0.03125 to 0.03125
- basis_g: bfloat16 [16384, 2048], P(('group', 'inp')), parts along dimension 0, may hold values from -0.0625 to 0.0625
- lengths: int32 [4], P(('group', 'out')), parts along dimension 0, may hold values from 128 to 512, as said below
Outputs:
- moments: float32 [4096, 4096], P(('group', 'out'), 'inp'), parts along dimension 0
The draws below stay inside these ranges and needn't reach their ends.
There are 2 independent parts, one for each index of `group`. The reference program is written for one: setup_inputs(seed, part) draws one part's arguments, and reference() takes and returns one part's arrays. A program takes and returns all parts, laid end to end along the dimension named above; each array names one. Nothing has to cross between parts.
Inputs may be any that keep to these rules, and one draw needn't show every extreme that they name: `lengths`: some sequence has all 512 tokens valid.
All inputs are finite; a program needn't handle non-finite values.
Results may differ from the reference program's by a relative error of at most 0.0042.
Values may be sent and summed in bfloat16 or wider, within the bound.
No kernel may reach another device: no remote copies, remote signals or barrier semaphores. Data moves between devices by JAX's collectives and lax.ppermute only.
A program may use at most 128 MiB of HBM per device.

```python
import jax
import jax.numpy as jnp

IN = 28672
OUT = 8192
KA = 4096
KG = 2048
SEQ_LEN = 512
SEQS = 2


def draw_lengths(key, part):
    key = jax.random.fold_in(key, 7)
    first_key = jax.random.fold_in(key, 1)
    second_key = jax.random.fold_in(key, 2)
    counts = jax.random.randint(first_key, (SEQS,), SEQ_LEN // 4, SEQ_LEN + 1)
    chosen = jax.random.randint(second_key, (), 0, SEQS)
    slots = jnp.arange(SEQS, dtype=jnp.int32)
    return jnp.where(slots == chosen, SEQ_LEN, counts).astype(jnp.int32)


def levels(stream_key, extent, split, smallest, largest):
    gain, own = 1.0, jax.random.fold_in(stream_key, 6)
    for axis_at, blocks in split:
        heights = jnp.exp(jax.random.uniform(jax.random.fold_in(own, axis_at), (blocks,), jnp.float32, smallest / len(split), largest / len(split)))
        gain = gain * jnp.repeat(heights, extent[axis_at] // blocks).reshape([-1 if axis == axis_at else 1 for axis in range(len(extent))])
    return gain


def bell_draw(own_key, shape, spread, most, split=(), kind=jnp.bfloat16):
    level = levels(own_key, shape, split, -0.22, 0.18) if split else 1.0
    entries = jax.random.normal(own_key, shape, jnp.float32) * spread * level
    return jnp.minimum(jnp.maximum(entries, -most), most).astype(kind)


def setup_inputs(seed: int = 0, part: int = 0) -> dict:
    seeds = jax.random.split(jax.random.key(seed), 6)
    part_keys = jax.random.split(jax.random.fold_in(seeds[5], part), 6)
    return {
        "acts": bell_draw(part_keys[0], (SEQS, SEQ_LEN, IN), 1.0, 6.0, ((0, 2), (2, 8))),
        "grads": bell_draw(part_keys[1], (SEQS, SEQ_LEN, OUT), 1.0, 6.0, ((0, 2), (2, 8))),
        "basis_a": bell_draw(part_keys[2], (IN, KA), IN ** -0.5, 0.03125, ((0, 8),)),
        "basis_g": bell_draw(part_keys[3], (OUT, KG), OUT ** -0.5, 0.0625, ((0, 8),)),
        "lengths": draw_lengths(jax.random.fold_in(jax.random.fold_in(seeds[5], part), 71), part),
    }


def reference(acts, grads, basis_a, basis_g, lengths):
    scale = 1.0 / (SEQ_LEN ** 0.5)
    summed = jnp.zeros((KG, KA), jnp.float32)
    positions = jnp.arange(SEQ_LEN, dtype=jnp.int32)
    for seq_index in range(SEQS):
        act_rot = jnp.dot(acts[seq_index], basis_a, preferred_element_type=jnp.float32).astype(jnp.bfloat16)
        grad_rot = jnp.dot(grads[seq_index], basis_g, preferred_element_type=jnp.float32).astype(jnp.bfloat16)
        valid = positions < lengths[seq_index]
        grad_valid = jnp.where(valid[:, None], grad_rot, jnp.zeros_like(grad_rot))
        rotated = jnp.dot(grad_valid.T, act_rot, preferred_element_type=jnp.float32) * scale
        summed = summed + rotated * rotated
    return summed / SEQS
```

```python
import functools

import jax
import jax.numpy as jnp
from jax import lax
from jax.experimental import pallas as pl
from jax.experimental.pallas import tpu as pltpu
from jax.sharding import PartitionSpec as P

SEQ_LEN = 512
SEQS = 2
TOKEN_CHUNKS = 2
LANES = 128
WIDTH = 256
ROUNDED_STEPS = 2


def reversed_bits(value, bits):
    return sum(((value >> bit) & 1) << (bits - 1 - bit) for bit in range(bits))


def rotate_kernel(order_ref, x_ref, *refs, columns, chunks, sent):
    del order_ref
    basis_refs = refs[:columns]
    send_refs = refs[columns : columns + chunks]
    keep_refs = refs[columns + chunks :]
    basis = jnp.concatenate([ref[...] for ref in basis_refs], axis=1)
    rotated = jnp.dot(x_ref[...], basis, preferred_element_type=jnp.float32)
    rows = rotated.shape[0] // chunks
    step = pl.program_id(0)

    @pl.when(step < sent)
    def _():
        for chunk, ref in enumerate(send_refs):
            ref[0] = rotated[chunk * rows : (chunk + 1) * rows].astype(ref.dtype)

    @pl.when(step >= sent)
    def _():
        for chunk, ref in enumerate(keep_refs):
            ref[0] = rotated[chunk * rows : (chunk + 1) * rows]


def rotate(order, x, basis, width, starts, stride):
    tokens, features = x.shape
    slices = order.shape[0]
    sent = slices // 2
    rows = tokens // TOKEN_CHUNKS
    wide = width * len(starts)

    def column_spec(start):
        return pl.BlockSpec((features, width), lambda step, order: (0, order[step] * stride + start))

    send_spec = pl.BlockSpec((1, rows, wide), lambda step, order: (jnp.minimum(step, sent - 1), 0, 0))
    keep_spec = pl.BlockSpec((1, rows, wide), lambda step, order: (jnp.maximum(step - sent, 0), 0, 0))
    send_shape = jax.ShapeDtypeStruct((sent, rows, wide), jnp.bfloat16)
    keep_shape = jax.ShapeDtypeStruct((sent, rows, wide), jnp.float32)
    outs = pl.pallas_call(
        functools.partial(rotate_kernel, columns=len(starts), chunks=TOKEN_CHUNKS, sent=sent),
        grid_spec=pltpu.PrefetchScalarGridSpec(
            num_scalar_prefetch=1,
            grid=(slices,),
            in_specs=[pl.BlockSpec((tokens, features), lambda step, order: (0, 0))]
            + [column_spec(start) for start in starts],
            out_specs=[send_spec] * TOKEN_CHUNKS + [keep_spec] * TOKEN_CHUNKS,
        ),
        out_shape=[send_shape] * TOKEN_CHUNKS + [keep_shape] * TOKEN_CHUNKS,
        compiler_params=pltpu.CompilerParams(vmem_limit_bytes=32 * 2**20),
        cost_estimate=pl.CostEstimate(
            flops=2 * tokens * features * wide * slices,
            bytes_accessed=2 * features * (wide * slices + tokens) + 6 * tokens * wide * slices // 2,
            transcendentals=0,
        ),
    )(order, x, *[basis] * len(starts))
    return list(zip(outs[:TOKEN_CHUNKS], outs[TOKEN_CHUNKS:]))


def rotate_narrow(order, x, basis, width, halves):
    tokens = x.shape[0]
    slices = order.shape[0]
    sent = slices // 2
    rows = tokens // TOKEN_CHUNKS
    rotated = jnp.dot(x, basis, preferred_element_type=jnp.float32)
    rotated = rotated.reshape(tokens, halves, slices, width).transpose(2, 0, 1, 3)
    rotated = jnp.take(rotated, order, axis=0).reshape(slices, tokens, halves * width)
    return [
        (
            rotated[:sent, chunk * rows : (chunk + 1) * rows].astype(jnp.bfloat16),
            rotated[sent:, chunk * rows : (chunk + 1) * rows],
        )
        for chunk in range(TOKEN_CHUNKS)
    ]


def swap(x, n, bit):
    return lax.ppermute(x, "inp", [(index, index ^ (1 << bit)) for index in range(n)])


def swap_cores(x):
    return lax.ppermute(x, "out", [(0, 1), (1, 0)])


def reduce_slices(send, keep, n, bits):
    for bit in range(bits):
        total = keep + swap(send, n, bit).astype(jnp.float32)
        half = total.shape[0] // 2
        if bit + 1 < bits:
            send, keep = total[:half], total[half:]
            if bit + 1 < ROUNDED_STEPS:
                send = send.astype(jnp.bfloat16)
    return total[0]


def gather_pieces(piece, n, bits):
    held = [piece[None]]
    for bit in reversed(range(bits)):
        held.append(swap(jnp.concatenate(held, axis=0) if len(held) > 1 else held[0], n, bit))
    return held


def moments_kernel(place_ref, *refs, sizes, chunks, blocks):
    groups = len(sizes)
    grad_refs = [refs[chunk * groups : (chunk + 1) * groups] for chunk in range(chunks)]
    act_refs = refs[chunks * groups : -1]
    out_ref = refs[-1]
    scale = 1.0 / SEQ_LEN**0.5
    wide = act_refs[0].shape[1]
    for block in range(blocks):
        high, low = [], []
        for seq in range(SEQS):
            act = jnp.concatenate(
                [act_refs[(block * chunks + chunk) * SEQS + seq][...] for chunk in range(chunks)], axis=0
            )
            high.append(act.astype(jnp.bfloat16))
            low.append((act - high[seq].astype(jnp.float32)).astype(jnp.bfloat16))
        position = 0
        for group, size in enumerate(sizes):
            rows = grad_refs[0][group].shape[2]
            total = None
            for seq in range(SEQS):
                grad = jnp.concatenate(
                    [
                        grad_refs[chunk][group][:, seq].reshape(size * rows, -1)
                        for chunk in range(chunks)
                    ],
                    axis=1,
                )
                rotated = jnp.dot(grad, high[seq], preferred_element_type=jnp.float32)
                rotated = rotated + jnp.dot(grad, low[seq], preferred_element_type=jnp.float32)
                rotated = rotated * scale
                squared = rotated * rotated
                total = squared if total is None else total + squared
            total = total / SEQS
            for index in range(size):
                start = pl.multiple_of(place_ref[position] * rows, rows)
                out_ref[pl.ds(start, rows), block * wide : (block + 1) * wide] = total[
                    index * rows : (index + 1) * rows
                ]
                position += 1


def second_moments(place, grad_pieces, acts, n):
    sizes = tuple(x.shape[0] for x in grad_pieces[0])
    rows = grad_pieces[0][0].shape[2]
    blocks = len(acts)
    wide = acts[0][0][0].shape[1]
    flat_grads = [x for chunk in grad_pieces for x in chunk]
    flat_acts = [x for block in acts for chunk in block for x in chunk]
    vmem = pl.BlockSpec(memory_space=pltpu.VMEM)
    return pl.pallas_call(
        functools.partial(moments_kernel, sizes=sizes, chunks=TOKEN_CHUNKS, blocks=blocks),
        out_shape=jax.ShapeDtypeStruct((n * rows, blocks * wide), jnp.float32),
        in_specs=[pl.BlockSpec(memory_space=pltpu.SMEM)] + [vmem] * (len(flat_grads) + len(flat_acts)),
        out_specs=vmem,
        compiler_params=pltpu.CompilerParams(vmem_limit_bytes=32 * 2**20),
        cost_estimate=pl.CostEstimate(
            flops=4 * SEQS * n * rows * blocks * wide * SEQ_LEN,
            bytes_accessed=4 * n * rows * blocks * wide + 4 * SEQS * SEQ_LEN * blocks * wide + 2 * SEQS * SEQ_LEN * n * rows,
            transcendentals=0,
        ),
    )(place, *flat_grads, *flat_acts)


def on_device(acts, grads, basis_a, basis_g, lengths, *, n):
    bits = n.bit_length() - 1
    me = lax.axis_index("inp")
    core = lax.axis_index("out")
    order = jnp.array([reversed_bits(n - 1 - at, bits) for at in range(n)], jnp.int32) ^ me
    place = jnp.array([reversed_bits(at, bits) for at in range(n)], jnp.int32) ^ me
    x_a, x_g = acts[0], grads[0]
    tokens = x_a.shape[0]
    rows = tokens // TOKEN_CHUNKS
    width_a = basis_a.shape[1] // n
    width_g = basis_g.shape[1] // n // 2

    if width_g % LANES == 0:
        parts_g = rotate(order, x_g, basis_g, width_g, (0, n), 1)
    else:
        parts_g = rotate_narrow(order, x_g, basis_g, width_g, 2)
    wide = min(WIDTH, width_a)
    blocks = width_a // wide
    parts_a = [rotate(order, x_a, basis_a, wide, (block,), blocks) for block in range(blocks)]

    grad_pieces = []
    for chunk, (send, keep) in enumerate(parts_g):
        grad_rot = reduce_slices(send, keep, n, bits).astype(jnp.bfloat16)
        positions = chunk * rows + lax.broadcasted_iota(jnp.int32, (rows, 1), 0)
        grad_valid = jnp.where(positions < lengths[0], grad_rot, jnp.zeros_like(grad_rot))
        grad_valid = grad_valid.T.reshape(2, width_g, rows)
        own = lax.dynamic_index_in_dim(grad_valid, core, 0, keepdims=False)
        other = lax.dynamic_index_in_dim(grad_valid, 1 - core, 0, keepdims=False)
        grad_pieces.append(gather_pieces(jnp.stack([own, swap_cores(other)]), n, bits))

    act_blocks = []
    for block in range(blocks):
        chunks = []
        for send, keep in parts_a[block]:
            act_rot = reduce_slices(send, keep, n, bits)
            chunks.append((act_rot, swap_cores(act_rot)))
        act_blocks.append(chunks)
    return second_moments(place, grad_pieces, act_blocks, n)


def solution(mesh):
    in_specs = (
        P(("group", "out"), None, "inp"),
        P(("group", "out"), None, "inp"),
        P(("group", "inp"), None),
        P(("group", "inp"), None),
        P(("group", "out")),
    )
    out_specs = P(("group", "out"), "inp")
    return jax.shard_map(
        functools.partial(on_device, n=mesh.shape["inp"]),
        mesh=mesh,
        in_specs=in_specs,
        out_specs=out_specs,
        check_vma=False,
    )
```

```python
import functools

import jax
import jax.numpy as jnp
from jax import lax
from jax.experimental import pallas as pl
from jax.experimental.pallas import tpu as pltpu
from jax.sharding import PartitionSpec as P

SEQ_LEN = 512
SEQS = 2
TOKEN_CHUNKS = 2
LANES = 128
WIDTH = 256
ROUNDED_STEPS_G = 2
ROUNDED_STEPS_A = 3
ANY = pl.BlockSpec(memory_space=pl.ANY)
VMEM = pl.BlockSpec(memory_space=pltpu.VMEM)
SMEM = pl.BlockSpec(memory_space=pltpu.SMEM)
MIB = 2**20
LIGHT = pl.CostEstimate(flops=0, bytes_accessed=0, transcendentals=0)


def reversed_bits(value, bits):
    return sum(((value >> bit) & 1) << (bits - 1 - bit) for bit in range(bits))


class Chain:
    def __init__(self):
        self.last = []
        self.clock = 0.0
        self.expected = []

    def expect(self, array, wait):
        self.expected.append((self.clock + wait, array))
        return array

    def waited_for(self):
        arrived = [array for due, array in self.expected if due <= self.clock]
        self.expected = [(due, array) for due, array in self.expected if due > self.clock]
        return self.last + arrived

    def call(self, body, out_shape, inputs, specs, out_specs=None, scratch=(), limit=12 * MIB, aliases=None):
        unread = self.waited_for()
        deps = len(unread)

        def kernel(*refs):
            body(*refs[: len(inputs)], *refs[len(inputs) + deps :])

        outs = pl.pallas_call(
            kernel,
            out_shape=out_shape,
            in_specs=list(specs) + [ANY] * deps,
            out_specs=out_specs or [VMEM] * len(out_shape),
            scratch_shapes=scratch,
            input_output_aliases=aliases or {},
            compiler_params=pltpu.CompilerParams(vmem_limit_bytes=limit),
            cost_estimate=LIGHT,
        )(*inputs, *unread)
        self.last = [outs[0]]
        return outs

    def rotate(self, order, x, basis, width, starts, stride, per_step, dtype):
        tokens, features = x.shape
        count = order.shape[0]
        rows = tokens // TOKEN_CHUNKS
        pieces = len(starts)
        wide = width * pieces
        unread = self.waited_for()
        deps = len(unread)

        def kernel(order_ref, x_ref, *refs):
            del order_ref
            columns = jnp.concatenate([ref[...] for ref in refs[: per_step * pieces]], axis=1)
            rotated = jnp.dot(x_ref[...], columns, preferred_element_type=jnp.float32)
            for at in range(per_step):
                for chunk, ref in enumerate(refs[per_step * pieces + deps :]):
                    ref[at] = rotated[
                        chunk * rows : (chunk + 1) * rows, at * wide : (at + 1) * wide
                    ].astype(ref.dtype)

        def column_spec(at, start):
            return pl.BlockSpec(
                (features, width), lambda step, order: (0, order[step * per_step + at] * stride + start)
            )

        column_specs = [column_spec(at, start) for at in range(per_step) for start in starts]
        outs = pl.pallas_call(
            kernel,
            grid_spec=pltpu.PrefetchScalarGridSpec(
                num_scalar_prefetch=1,
                grid=(count // per_step,),
                in_specs=[pl.BlockSpec((tokens, features), lambda step, order: (0, 0))] + column_specs + [ANY] * deps,
                out_specs=[pl.BlockSpec((per_step, rows, wide), lambda step, order: (step, 0, 0))] * TOKEN_CHUNKS,
            ),
            out_shape=[jax.ShapeDtypeStruct((count, rows, wide), dtype)] * TOKEN_CHUNKS,
            compiler_params=pltpu.CompilerParams(vmem_limit_bytes=32 * MIB),
            cost_estimate=LIGHT,
        )(order, x, *[basis] * len(column_specs), *unread)
        self.last = [outs[0]]
        return outs

    def combine(self, received, kept, dtype):
        count, rows, wide = kept.shape
        half = count // 2

        def body(received_ref, kept_ref, send_ref, hold_ref):
            send_ref[...] = (kept_ref[:half] + received_ref[:half].astype(jnp.float32)).astype(send_ref.dtype)
            hold_ref[...] = kept_ref[half:] + received_ref[half:].astype(jnp.float32)

        return self.call(
            body,
            [
                jax.ShapeDtypeStruct((half, rows, wide), dtype),
                jax.ShapeDtypeStruct((half, rows, wide), jnp.float32),
            ],
            [received, kept],
            [VMEM] * 2,
        )

    def finish(self, received, kept):
        rows, wide = kept[0].shape[1:]

        def body(*refs):
            out_ref = refs[-1]
            for chunk in range(TOKEN_CHUNKS):
                total = refs[TOKEN_CHUNKS + chunk][0] + refs[chunk][0].astype(jnp.float32)
                out_ref[chunk * rows : (chunk + 1) * rows] = total

        shape = jax.ShapeDtypeStruct((rows * TOKEN_CHUNKS, wide), jnp.float32)
        return self.call(body, [shape], [*received, *kept], [VMEM] * (2 * TOKEN_CHUNKS))[0]

    def finish_grads(self, scalars, received, kept):
        rows, wide = kept[0].shape[1:]
        half = wide // 2

        def body(scalars_ref, *refs):
            columns = []
            for chunk in range(TOKEN_CHUNKS):
                total = refs[TOKEN_CHUNKS + chunk][0] + refs[chunk][0].astype(jnp.float32)
                positions = chunk * rows + lax.broadcasted_iota(jnp.int32, (rows, wide), 0)
                total = jnp.where(positions < scalars_ref[0], total, jnp.zeros_like(total))
                columns.append(total.T.astype(jnp.bfloat16))
            grad = jnp.concatenate(columns, axis=1)
            mine_ref, other_ref = refs[2 * TOKEN_CHUNKS :]

            @pl.when(scalars_ref[1] == 0)
            def _():
                mine_ref[...] = grad[:half]
                other_ref[...] = grad[half:]

            @pl.when(scalars_ref[1] != 0)
            def _():
                mine_ref[...] = grad[half:]
                other_ref[...] = grad[:half]

        shape = jax.ShapeDtypeStruct((half, rows * TOKEN_CHUNKS), jnp.bfloat16)
        return self.call(
            body, [shape] * 2, [scalars, *received, *kept], [SMEM] + [VMEM] * (2 * TOKEN_CHUNKS)
        )

    def pair(self, mine, other):
        def body(mine_ref, other_ref, out_ref):
            out_ref[0, 0] = mine_ref[...]
            out_ref[0, 1] = other_ref[...]

        shape = jax.ShapeDtypeStruct((1, 2) + mine.shape, mine.dtype)
        return self.call(body, [shape], [mine, other], [VMEM] * 2)[0]

    def join(self, held, received):
        count = held.shape[0]

        def body(held_ref, received_ref, out_ref):
            out_ref[:count] = held_ref[...]
            out_ref[count:] = received_ref[...]

        shape = jax.ShapeDtypeStruct((2 * count,) + held.shape[1:], held.dtype)
        return self.call(body, [shape], [held, received], [VMEM] * 2)[0]

    def moments(self, place, grads, acts, out_shape, earlier=None):
        rows, tokens = grads[0].shape[2:]
        count = sum(x.shape[0] for x in grads)
        blocks = len(acts)
        flat_acts = [x for block in acts for x in block]
        scale = 1.0 / SEQ_LEN**0.5

        def body(place_ref, *refs):
            grad_refs = refs[: len(grads)]
            act_refs = refs[len(grads) : len(grads) + len(flat_acts)]
            out_ref, result_ref, sems = refs[-3:]
            total = None
            for seq in range(SEQS):
                act = jnp.concatenate([act_refs[block * SEQS + seq][...] for block in range(blocks)], axis=1)
                high = act.astype(jnp.bfloat16)
                low = (act - high.astype(jnp.float32)).astype(jnp.bfloat16)
                grad = jnp.concatenate([ref[:, seq].reshape(-1, tokens) for ref in grad_refs], axis=0)
                rotated = jnp.dot(grad, high, preferred_element_type=jnp.float32)
                rotated = rotated + jnp.dot(grad, low, preferred_element_type=jnp.float32)
                rotated = rotated * scale
                squared = rotated * rotated
                total = squared if total is None else total + squared
            result_ref[...] = total / SEQS
            copies = []
            for at in range(count):
                start = pl.multiple_of(place_ref[at] * rows, rows)
                copies.append(
                    pltpu.make_async_copy(
                        result_ref.at[pl.ds(at * rows, rows)], out_ref.at[pl.ds(start, rows)], sems.at[at]
                    )
                )
                copies[-1].start()
            for copy in copies:
                copy.wait()

        inputs = [place, *grads, *flat_acts]
        specs = [SMEM] + [VMEM] * (len(inputs) - 1)
        aliases = {}
        if earlier is not None:
            aliases = {len(inputs): 0}
            inputs.append(earlier)
            specs.append(ANY)
        return self.call(
            body,
            [out_shape],
            inputs,
            specs,
            out_specs=[ANY],
            scratch=[
                pltpu.VMEM((count * rows, out_shape.shape[1]), jnp.float32),
                pltpu.SemaphoreType.DMA((count,)),
            ],
            limit=24 * MIB,
            aliases=aliases,
        )[0]


def rotate_narrow(order, x, basis, width, halves, slices, dtype):
    tokens = x.shape[0]
    rows = tokens // TOKEN_CHUNKS
    rotated = jnp.dot(x, basis, preferred_element_type=jnp.float32)
    rotated = rotated.reshape(tokens, halves, slices, width).transpose(2, 0, 1, 3)
    rotated = jnp.take(rotated, order, axis=0).reshape(-1, tokens, halves * width).astype(dtype)
    return [rotated[:, chunk * rows : (chunk + 1) * rows] for chunk in range(TOKEN_CHUNKS)]


def swap(x, n, bit):
    return lax.ppermute(x, "inp", [(index, index ^ (1 << bit)) for index in range(n)])


def swap_cores(x):
    return lax.ppermute(x, "out", [(0, 1), (1, 0)])


def on_device(acts, grads, basis_a, basis_g, lengths, *, n):
    bits = n.bit_length() - 1
    me = lax.axis_index("inp")
    core = lax.axis_index("out")
    order = jnp.array([reversed_bits(n - 1 - at, bits) for at in range(n)], jnp.int32) ^ me
    orders = (order[: n // 2], order[n // 2 :])
    scalars = jnp.stack([lengths[0], core]).astype(jnp.int32)
    x_a, x_g = acts[0], grads[0]
    width_a = basis_a.shape[1] // n
    width_g = basis_g.shape[1] // n // 2
    wide = min(WIDTH, width_a)
    blocks = width_a // wide
    chain = Chain()

    sending, kept, received, finished = {}, {}, {}, {}
    grad_keys = [("g", 0, chunk) for chunk in range(TOKEN_CHUNKS)]
    act_keys = [("a", block, chunk) for block in range(blocks) for chunk in range(TOKEN_CHUNKS)]

    def rotate_grads(part):
        dtype = (jnp.bfloat16, jnp.float32)[part]
        if width_g % LANES == 0:
            outs = chain.rotate(orders[part], x_g, basis_g, width_g, (0, n), 1, 2, dtype)
        else:
            outs = rotate_narrow(orders[part], x_g, basis_g, width_g, 2, n, dtype)
        for key, x in zip(grad_keys, outs):
            if part == 0:
                received[key] = swap(x, n, 0)
            else:
                kept[key] = x

    def rotate_acts(block, part):
        dtype = (jnp.bfloat16, jnp.float32)[part]
        outs = chain.rotate(orders[part], x_a, basis_a, wide, (block,), blocks, 2, dtype)
        for chunk, x in enumerate(outs):
            if part == 0:
                received["a", block, chunk] = swap(x, n, 0)
            else:
                kept["a", block, chunk] = x

    def advance(key, step):
        rounded = ROUNDED_STEPS_G if key[0] == "g" else ROUNDED_STEPS_A
        dtype = jnp.bfloat16 if step + 1 < rounded else jnp.float32
        send, kept[key] = chain.combine(received[key], kept[key], dtype)
        wait = (0.8 if dtype == jnp.bfloat16 else 1.05) if step else 0.56
        received[key] = chain.expect(swap(send, n, step + 1), wait)

    def finish_acts(block):
        keys = [("a", block, chunk) for chunk in range(TOKEN_CHUNKS)]
        own = chain.finish([received[key] for key in keys], [kept[key] for key in keys])
        finished[block] = (own, chain.expect(swap_cores(own), 0.2))

    gathered = {}

    def finish_grads():
        mine, other = chain.finish_grads(
            scalars, [received[key] for key in grad_keys], [kept[key] for key in grad_keys]
        )
        gathered["mine"], gathered["other"] = mine, swap_cores(other)

    def pair_grads():
        gathered["held"] = chain.pair(gathered["mine"], gathered["other"])
        gathered["order"] = [0]
        gathered["in"] = swap(gathered["held"], n, bits - 1)

    def join_grads(bit):
        gathered["held"] = chain.join(gathered["held"], gathered["in"])
        gathered["order"] = gathered["order"] + [at ^ (1 << bit) for at in gathered["order"]]
        gathered["in"] = swap(gathered["held"], n, bit - 1)
        if bit == 2:
            gathered["side"] = chain.expect(swap(gathered["held"], n, 0), 1.7)

    def relay_grads():
        chain.last.append(gathered["in"])
        gathered["across"] = swap(gathered["in"], n, 0)

    tasks = [(-2.0, rotate_grads, (0,)), (-1.0, rotate_grads, (1,))]
    for block in range(blocks):
        tasks.append((0.1 + 1.0 * block, rotate_acts, (block, 0)))
        tasks.append((2.1 + 2.2 * block, rotate_acts, (block, 1)))
    for at, key in enumerate(grad_keys + act_keys):
        pace = 0.55 if key in (grad_keys[-1], act_keys[-1]) else 1.01
        for step in range(bits - 1):
            tasks.append((1.0 + at + pace * step, advance, (key, step)))
        if key in act_keys and key[2] == TOKEN_CHUNKS - 1:
            tasks.append((1.0 + at + pace * (bits - 1) + 0.01, finish_acts, (key[1],)))
    clock = TOKEN_CHUNKS + 0.55 * (bits - 1) + 0.95
    tasks.append((clock, finish_grads, ()))
    clock += 0.15
    tasks.append((clock, pair_grads, ()))
    for bit in range(bits - 1, 1, -1):
        clock += 1.1
        tasks.append((clock, join_grads, (bit,)))
    tasks.append((clock + 1.0, relay_grads, ()))
    for chain.clock, task, arguments in sorted(tasks, key=lambda task: task[0]):
        task(*arguments)

    low = gathered["order"]
    offsets = low + [at ^ 2 for at in low] + [at ^ 1 for at in low] + [at ^ 3 for at in low]
    place = jnp.array(offsets, jnp.int32) ^ me
    act_blocks = [finished[block] for block in range(blocks)]
    first = 3 * len(low)
    out_shape = jax.ShapeDtypeStruct((n * width_g, width_a), jnp.float32)
    out = chain.moments(
        place[:first], [gathered["held"], gathered["in"], gathered["side"]], act_blocks, out_shape
    )
    chain.last = []
    return chain.moments(place[first:], [gathered["across"]], act_blocks, out_shape, earlier=out)


def solution(mesh):
    in_specs = (
        P(("group", "out"), None, "inp"),
        P(("group", "out"), None, "inp"),
        P(("group", "inp"), None),
        P(("group", "inp"), None),
        P(("group", "out")),
    )
    out_specs = P(("group", "out"), "inp")
    return jax.shard_map(
        functools.partial(on_device, n=mesh.shape["inp"]),
        mesh=mesh,
        in_specs=in_specs,
        out_specs=out_specs,
        check_vma=False,
    )
```

```python
import functools

import jax
import jax.numpy as jnp
from jax import lax
from jax.experimental import pallas as pl
from jax.experimental.pallas import tpu as pltpu
from jax.sharding import PartitionSpec as P

SEQ_LEN = 512
SEQS = 2
TOKEN_CHUNKS = 2
LANES = 128
WIDTH = 256
ROUNDED_STEPS = {"g": 2, "a": 3}
ANY = pl.BlockSpec(memory_space=pl.ANY)
CODE_ROWS = 16
CODE_TOP = 2.0**15
CODE_LEAST = 2.0**-100
VMEM = pl.BlockSpec(memory_space=pltpu.VMEM)
SMEM = pl.BlockSpec(memory_space=pltpu.SMEM)
MIB = 2**20
LIGHT = pl.CostEstimate(flops=0, bytes_accessed=2**17, transcendentals=0)


SEND_AT = (9.0, 22.0)
KEEP_AT = (31.0, 46.0)
GRAD_STEPS_AT = ((17.0, 29.0), (18.0, 30.0))
ACT_STEPS_AT = ((51.0, 66.0, 76.0, 90.0), (74.0, 83.0, 89.2, 97.8))
GRADS_AT = 44.0
RELAY_WAIT = 30.0
ACROSS_WAIT = 24.0
BEHIND = {
    ("a", 0): (("g", 1), 0),
}


def decode(ref, rows):
    arrived = ref[...].astype(jnp.float32)
    if arrived.shape[1] == rows:
        return arrived
    return arrived[:, :rows] * jnp.exp2(-arrived[:, rows : rows + 1])


class Chain:
    def __init__(self):
        self.last = []
        self.clock = 0.0
        self.expected = []

    def expect(self, array, wait):
        self.expected.append((self.clock + wait, array))
        return array

    def waited_for(self):
        arrived = [array for due, array in self.expected if due <= self.clock]
        self.expected = [(due, array) for due, array in self.expected if due > self.clock]
        return self.last + arrived

    def call(self, body, out_shape, inputs, specs, out_specs=None, scratch=(), limit=12 * MIB, aliases=None, carry=()):
        unread = self.waited_for()
        deps = len(unread)

        carried = len(carry)
        aliases = dict(aliases or {})
        for at in range(carried):
            aliases[len(inputs) + deps + at] = len(out_shape) + at

        def kernel(*refs):
            rest = refs[len(inputs) + deps + carried :]
            body(*refs[: len(inputs)], *rest[: len(out_shape)], *rest[len(out_shape) + carried :])

        outs = pl.pallas_call(
            kernel,
            out_shape=list(out_shape) + [jax.ShapeDtypeStruct(x.shape, x.dtype) for x in carry],
            in_specs=list(specs) + [ANY] * (deps + carried),
            out_specs=(out_specs or [VMEM] * len(out_shape)) + [ANY] * carried,
            scratch_shapes=scratch,
            input_output_aliases=aliases,
            compiler_params=pltpu.CompilerParams(vmem_limit_bytes=limit),
            cost_estimate=LIGHT,
        )(*inputs, *unread, *carry)
        self.last = [outs[0]]
        return outs

    def rotate(self, order, x, basis, width, start, stride, per_step, chunks, dtype, limit=32 * MIB):
        tokens, features = x.shape
        count = order.shape[0]
        rows = tokens // chunks
        unread = self.waited_for()
        deps = len(unread)

        def kernel(order_ref, x_ref, *refs):
            del order_ref
            columns = jnp.concatenate([ref[...] for ref in refs[:per_step]], axis=1)
            rotated = jnp.dot(x_ref[...], columns, preferred_element_type=jnp.float32)
            for at in range(per_step):
                for chunk, ref in enumerate(refs[per_step + deps :]):
                    ref[at] = rotated[
                        chunk * rows : (chunk + 1) * rows, at * width : (at + 1) * width
                    ].astype(ref.dtype)

        def column_spec(at):
            return pl.BlockSpec(
                (features, width), lambda step, order: (0, order[step * per_step + at] * stride + start)
            )

        outs = pl.pallas_call(
            kernel,
            grid_spec=pltpu.PrefetchScalarGridSpec(
                num_scalar_prefetch=1,
                grid=(count // per_step,),
                in_specs=[pl.BlockSpec((tokens, features), lambda step, order: (0, 0))]
                + [column_spec(at) for at in range(per_step)]
                + [ANY] * deps,
                out_specs=[pl.BlockSpec((per_step, rows, width), lambda step, order: (step, 0, 0))] * chunks,
            ),
            out_shape=[jax.ShapeDtypeStruct((count, rows, width), dtype)] * chunks,
            compiler_params=pltpu.CompilerParams(vmem_limit_bytes=limit),
            cost_estimate=LIGHT,
        )(order, x, *[basis] * per_step, *unread)
        self.last = [outs[0]]
        return outs

    def combine(self, received, kept, dtype, parts=1, carry=()):
        count, rows, wide = kept.shape
        part_rows = rows // parts
        half = count // 2
        coded = dtype == jnp.float16

        def body(received_ref, kept_ref, *refs):
            arrived = decode(received_ref, rows)
            for part in range(parts):
                send_ref, hold_ref = refs[part], refs[parts + part]
                at = slice(part * part_rows, (part + 1) * part_rows)
                total = kept_ref[:half, at] + arrived[:half, at]
                hold_ref[...] = kept_ref[half:, at] + arrived[half:, at]
                if coded:
                    largest = jnp.full((half, CODE_ROWS, wide), jnp.max(jnp.abs(total)))
                    exponent = jnp.floor(jnp.log2(CODE_TOP / jnp.maximum(largest, CODE_LEAST)))
                    send_ref[:, :part_rows] = total * jnp.exp2(exponent[:, :1])
                    send_ref[:, part_rows:] = exponent
                else:
                    send_ref[...] = total.astype(send_ref.dtype)

        send_shape = (half, part_rows + CODE_ROWS * coded, wide)
        outs = self.call(
            body,
            [jax.ShapeDtypeStruct(send_shape, jnp.float32 if coded else dtype)] * parts
            + [jax.ShapeDtypeStruct((half, part_rows, wide), jnp.float32)] * parts,
            [received, kept],
            [VMEM] * 2,
            carry=carry,
        )
        return [x.astype(dtype) for x in outs[:parts]], outs[parts : 2 * parts], outs[2 * parts :]

    def finish(self, received, kept):
        rows, wide = kept[0].shape[1:]

        def body(*refs):
            out_ref = refs[-1]
            for chunk in range(TOKEN_CHUNKS):
                total = refs[TOKEN_CHUNKS + chunk][0] + refs[chunk][0].astype(jnp.float32)
                out_ref[chunk * rows : (chunk + 1) * rows] = total

        shape = jax.ShapeDtypeStruct((rows * TOKEN_CHUNKS, wide), jnp.float32)
        return self.call(body, [shape], [*received, *kept], [VMEM] * (2 * TOKEN_CHUNKS))[0]

    def finish_grads(self, scalars, received, kept):
        tokens, wide = kept[0].shape[1:]

        def body(scalars_ref, *refs):
            positions = lax.broadcasted_iota(jnp.int32, (tokens, wide), 0)
            valid = positions < scalars_ref[0]

            def grad(core):
                total = refs[2 + core][0] + decode(refs[core], tokens)[0]
                total = jnp.where(valid, total, jnp.zeros_like(total))
                return total.T.astype(jnp.bfloat16)

            mine_ref, other_ref = refs[4:]

            @pl.when(scalars_ref[1] == 0)
            def _():
                mine_ref[...] = grad(0)
                other_ref[...] = grad(1)

            @pl.when(scalars_ref[1] != 0)
            def _():
                mine_ref[...] = grad(1)
                other_ref[...] = grad(0)

        shape = jax.ShapeDtypeStruct((wide, tokens), jnp.bfloat16)
        return self.call(body, [shape] * 2, [scalars, *received, *kept], [SMEM] + [VMEM] * 4)

    def pair(self, mine, other):
        def body(mine_ref, other_ref, out_ref):
            out_ref[0, 0] = mine_ref[...]
            out_ref[0, 1] = other_ref[...]

        shape = jax.ShapeDtypeStruct((1, 2) + mine.shape, mine.dtype)
        return self.call(body, [shape], [mine, other], [VMEM] * 2)[0]

    def relay(self, x):
        def body(out_ref):
            out_ref[...] = jnp.zeros_like(out_ref)

        return self.call(body, [jax.ShapeDtypeStruct((8, LANES), jnp.float32)], [], [], carry=[x])[1]

    def moments(self, place, grads, acts, out_shape):
        rows, tokens = grads[0].shape[2:]
        count = sum(x.shape[0] for x in grads)
        blocks = len(acts)
        flat_acts = [x for block in acts for x in block]
        scale = 1.0 / SEQ_LEN**0.5

        def body(place_ref, *refs):
            grad_refs = refs[: len(grads)]
            act_refs = refs[len(grads) : len(grads) + len(flat_acts)]
            out_ref, result_ref, sems = refs[-3:]
            total = None
            for seq in range(SEQS):
                act = jnp.concatenate([act_refs[block * SEQS + seq][...] for block in range(blocks)], axis=1)
                high = act.astype(jnp.bfloat16)
                low = (act - high.astype(jnp.float32)).astype(jnp.bfloat16)
                grad = jnp.concatenate([ref[:, seq].reshape(-1, tokens) for ref in grad_refs], axis=0)
                rotated = jnp.dot(grad, high, preferred_element_type=jnp.float32)
                rotated = rotated + jnp.dot(grad, low, preferred_element_type=jnp.float32)
                rotated = rotated * scale
                squared = rotated * rotated
                total = squared if total is None else total + squared
            result_ref[...] = total / SEQS
            copies = []
            for at in range(count):
                start = pl.multiple_of(place_ref[at] * rows, rows)
                copies.append(
                    pltpu.make_async_copy(
                        result_ref.at[pl.ds(at * rows, rows)], out_ref.at[pl.ds(start, rows)], sems.at[at]
                    )
                )
                copies[-1].start()
            for copy in copies:
                copy.wait()

        inputs = [place, *grads, *flat_acts]
        specs = [SMEM] + [VMEM] * (len(inputs) - 1)
        return self.call(
            body,
            [out_shape],
            inputs,
            specs,
            out_specs=[ANY],
            scratch=[
                pltpu.VMEM((count * rows, out_shape.shape[1]), jnp.float32),
                pltpu.SemaphoreType.DMA((count,)),
            ],
            limit=24 * MIB,
        )[0]


def rotate_narrow(order, x, basis, width, start, slices, dtype):
    columns = basis[:, start * width : (start + slices) * width]
    rotated = jnp.dot(x, columns, preferred_element_type=jnp.float32)
    rotated = rotated.reshape(x.shape[0], slices, width).transpose(1, 0, 2)
    return [jnp.take(rotated, order, axis=0).astype(dtype)]


def halving_order(n, steps):
    bits = len(steps)
    return [
        sum((1 - ((at >> (bits - 1 - step)) & 1)) << bit for step, bit in enumerate(steps)) for at in range(n)
    ]


def swap(x, n, bit):
    return lax.ppermute(x, "inp", [(index, index ^ (1 << bit)) for index in range(n)])


def swap_cores(x):
    return lax.ppermute(x, "out", [(0, 1), (1, 0)])


def on_device(acts, grads, basis_a, basis_g, lengths, *, n):
    bits = n.bit_length() - 1
    me = lax.axis_index("inp")
    core = lax.axis_index("out")
    scalars = jnp.stack([lengths[0], core]).astype(jnp.int32)
    x_a, x_g = acts[0], grads[0]
    width_a = basis_a.shape[1] // n
    width_g = basis_g.shape[1] // n // 2
    wide = min(WIDTH, width_a)
    blocks = width_a // wide
    chain = Chain()

    forward = list(range(bits))
    crossed = [1, 0] + forward[2:]
    grad_keys = [("g", 0), ("g", 1)]
    act_keys = [("a", block) for block in range(blocks)]
    steps_of = {key: forward for key in grad_keys + act_keys}
    steps_of["g", 0] = crossed
    orders = {}
    for steps in (forward, crossed):
        order = jnp.array(halving_order(n, steps), jnp.int32) ^ me
        orders[tuple(steps)] = (order[: n // 2], order[n // 2 :])
    kept, received, finished, gathered = {}, {}, {}, {}
    waiting, worked = {}, set()

    def at_work(task):
        return task not in worked

    def keep_or_send(key, x, part):
        if part == 0 and key in BEHIND and at_work(BEHIND[key]):
            waiting.setdefault(BEHIND[key], []).append((key, x))
        elif part == 0:
            received[key] = swap(x, n, steps_of[key][0])
        else:
            kept[key] = x

    def rotate_grads(half, part):
        key = ("g", half)
        order = orders[tuple(steps_of[key])][part]
        dtype = (jnp.bfloat16, jnp.float32)[part]
        if width_g % LANES == 0:
            (x,) = chain.rotate(order, x_g, basis_g, width_g, half * n, 1, order.shape[0] // 2, 1, dtype)
        else:
            (x,) = rotate_narrow(order, x_g, basis_g, width_g, half * n, n, dtype)
        keep_or_send(key, x, part)

    def rotate_acts(block, part):
        order = orders[tuple(forward)][part]
        dtype = (jnp.bfloat16, jnp.float32)[part]
        (x,) = chain.rotate(order, x_a, basis_a, wide, block, blocks, 2, 1, dtype)
        keep_or_send(("a", block), x, part)

    def advance(key, step, chunk=None):
        worked.add((key, step))
        wider = jnp.float16 if key[0] == "g" else jnp.float32
        dtype = jnp.bfloat16 if step + 1 < ROUNDED_STEPS[key[0]] else wider
        behind = waiting.pop((key, step), [])
        split = TOKEN_CHUNKS if key[0] == "a" and step == 0 else 1
        name = key if chunk is None else key + (chunk,)
        sends, holds, carried = chain.combine(received[name], kept[name], dtype, split, [x for _, x in behind])
        for (other, _), x in zip(behind, carried):
            received[other] = swap(x, n, steps_of[other][0])
        for part in range(split):
            name = key + (part,) if split > 1 else name
            arrived = swap(sends[part], n, steps_of[key][step + 1])
            received[name] = arrived.astype(jnp.float32) if dtype == jnp.float16 else arrived
            kept[name] = holds[part]

    def finish_acts(block):
        keys = [("a", block, chunk) for chunk in range(TOKEN_CHUNKS)]
        own = chain.finish([received[key] for key in keys], [kept[key] for key in keys])
        finished[block] = (own, chain.expect(swap_cores(own), 4.0))

    def finish_grads():
        mine, other = chain.finish_grads(
            scalars, [received[key] for key in grad_keys], [kept[key] for key in grad_keys]
        )
        gathered["mine"], gathered["other"] = mine, swap_cores(other)

    def pair_grads():
        held = chain.pair(gathered["mine"], gathered["other"])
        sides = [[at for at in range(n) if at % 2 == side] for side in range(2)]
        gathered["held"] = lax.all_gather(held, "inp", axis_index_groups=sides, tiled=True)

    def relay_grads():
        gathered["held"] = chain.relay(gathered["held"])
        gathered["across"] = chain.expect(swap(gathered["held"], n, 0), ACROSS_WAIT)

    tasks = [
        (0.0, rotate_grads, (0, 0)),
        (1.0, rotate_grads, (1, 0)),
        (2.0, rotate_grads, (0, 1)),
        (3.0, rotate_grads, (1, 1)),
    ]
    for block in range(blocks):
        tasks.append((SEND_AT[block], rotate_acts, (block, 0)))
        tasks.append((KEEP_AT[block], rotate_acts, (block, 1)))
    for key, times in zip(grad_keys, GRAD_STEPS_AT):
        for step in range(bits - 1):
            tasks.append((times[min(step, 1)] + 8.0 * max(step - 1, 0), advance, (key, step)))
    for key, times in zip(act_keys, ACT_STEPS_AT):
        tasks.append((times[0], advance, (key, 0)))
        for step in range(1, bits - 1):
            for chunk in range(TOKEN_CHUNKS):
                tasks.append((times[1 + chunk] + 8.0 * (step - 1), advance, (key, step, chunk)))
        tasks.append((times[-1] + 8.0 * (bits - 3), finish_acts, (key[1],)))
    clock = GRADS_AT + 8.0 * (bits - 3)
    tasks.append((clock, finish_grads, ()))
    clock += 1.0
    tasks.append((clock, pair_grads, ()))
    tasks.append((clock + RELAY_WAIT, relay_grads, ()))
    for chain.clock, task, arguments in sorted(tasks, key=lambda task: task[0]):
        task(*arguments)

    same_side = 2 * jnp.arange(n // 2, dtype=jnp.int32) + me % 2
    place = jnp.concatenate([same_side, same_side ^ 1])
    act_blocks = [finished[block] for block in range(blocks)]
    out_shape = jax.ShapeDtypeStruct((n * width_g, width_a), jnp.float32)
    grads = [gathered[name] for name in ("held", "across")]
    return chain.moments(place, grads, act_blocks, out_shape)


def solution(mesh):
    in_specs = (
        P(("group", "out"), None, "inp"),
        P(("group", "out"), None, "inp"),
        P(("group", "inp"), None),
        P(("group", "inp"), None),
        P(("group", "out")),
    )
    out_specs = P(("group", "out"), "inp")
    return jax.shard_map(
        functools.partial(on_device, n=mesh.shape["inp"]),
        mesh=mesh,
        in_specs=in_specs,
        out_specs=out_specs,
        check_vma=False,
    )
```

```python
import functools

import jax
import jax.numpy as jnp
from jax import lax
from jax.experimental import pallas as pl
from jax.experimental.pallas import tpu as pltpu
from jax.sharding import PartitionSpec as P

SEQ_LEN = 512
SEQS = 2
TOKEN_CHUNKS = 2
LANES = 128
WIDTH = 256
ROUNDED_STEPS = {"g": 2, "a": 3}
ANY = pl.BlockSpec(memory_space=pl.ANY)
CODE_ROWS = 16
CODE_TOP = 2.0**15
CODE_LEAST = 2.0**-100
VMEM = pl.BlockSpec(memory_space=pltpu.VMEM)
SMEM = pl.BlockSpec(memory_space=pltpu.SMEM)
MIB = 2**20
LIGHT = pl.CostEstimate(flops=0, bytes_accessed=2**17, transcendentals=0)


SEND_AT = (9.0, 43.0)
KEEP_AT = (22.0, 59.0)
STEPS_AT = ((21.0, 29.0), (30.0, 39.0), (42.0, 47.9), (48.5, 66.5), (66.2, 90.0), (74.0, 95.0))
FINISH_AT = (99.0, 100.0)
GRADS_AT = 48.0
JOIN_WAIT = 18.0
RELAY_WAIT = 14.0
SIDE_WAIT = 20.0
ACROSS_WAIT = 100.0
EXPECTED = {("g", 0): 9.5, ("a", 0, 0): 18.0, ("a", 0, 1): 28.0}


def decode(ref, rows):
    arrived = ref[...].astype(jnp.float32)
    if arrived.shape[1] == rows:
        return arrived
    return arrived[:, :rows] * jnp.exp2(-arrived[:, rows : rows + 1])


class Chain:
    def __init__(self):
        self.last = []
        self.clock = 0.0
        self.expected = []

    def expect(self, array, wait):
        self.expected.append((self.clock + wait, array))
        return array

    def waited_for(self):
        arrived = [array for due, array in self.expected if due <= self.clock]
        self.expected = [(due, array) for due, array in self.expected if due > self.clock]
        return self.last + arrived

    def call(self, body, out_shape, inputs, specs, out_specs=None, scratch=(), limit=12 * MIB, aliases=None, carry=()):
        unread = self.waited_for()
        deps = len(unread)

        carried = len(carry)
        aliases = dict(aliases or {})
        for at in range(carried):
            aliases[len(inputs) + deps + at] = len(out_shape) + at

        def kernel(*refs):
            rest = refs[len(inputs) + deps + carried :]
            body(*refs[: len(inputs)], *rest[: len(out_shape)], *rest[len(out_shape) + carried :])

        outs = pl.pallas_call(
            kernel,
            out_shape=list(out_shape) + [jax.ShapeDtypeStruct(x.shape, x.dtype) for x in carry],
            in_specs=list(specs) + [ANY] * (deps + carried),
            out_specs=(out_specs or [VMEM] * len(out_shape)) + [ANY] * carried,
            scratch_shapes=scratch,
            input_output_aliases=aliases,
            compiler_params=pltpu.CompilerParams(vmem_limit_bytes=limit),
            cost_estimate=LIGHT,
        )(*inputs, *unread, *carry)
        self.last = [outs[0]]
        return outs

    def rotate(self, order, x, basis, width, start, stride, per_step, chunks, dtype, limit=32 * MIB):
        tokens, features = x.shape
        count = order.shape[0]
        rows = tokens // chunks
        unread = self.waited_for()
        deps = len(unread)

        def kernel(order_ref, x_ref, *refs):
            del order_ref
            columns = jnp.concatenate([ref[...] for ref in refs[:per_step]], axis=1)
            rotated = jnp.dot(x_ref[...], columns, preferred_element_type=jnp.float32)
            for at in range(per_step):
                for chunk, ref in enumerate(refs[per_step + deps :]):
                    ref[at] = rotated[
                        chunk * rows : (chunk + 1) * rows, at * width : (at + 1) * width
                    ].astype(ref.dtype)

        def column_spec(at):
            return pl.BlockSpec(
                (features, width), lambda step, order: (0, order[step * per_step + at] * stride + start)
            )

        outs = pl.pallas_call(
            kernel,
            grid_spec=pltpu.PrefetchScalarGridSpec(
                num_scalar_prefetch=1,
                grid=(count // per_step,),
                in_specs=[pl.BlockSpec((tokens, features), lambda step, order: (0, 0))]
                + [column_spec(at) for at in range(per_step)]
                + [ANY] * deps,
                out_specs=[pl.BlockSpec((per_step, rows, width), lambda step, order: (step, 0, 0))] * chunks,
            ),
            out_shape=[jax.ShapeDtypeStruct((count, rows, width), dtype)] * chunks,
            compiler_params=pltpu.CompilerParams(vmem_limit_bytes=limit),
            cost_estimate=LIGHT,
        )(order, x, *[basis] * per_step, *unread)
        self.last = [outs[0]]
        return outs

    def combine(self, received, kept, dtype):
        count, rows, wide = kept.shape
        half = count // 2
        coded = dtype == jnp.float16

        def body(received_ref, kept_ref, send_ref, hold_ref):
            arrived = decode(received_ref, rows)
            total = kept_ref[:half] + arrived[:half]
            hold_ref[...] = kept_ref[half:] + arrived[half:]
            if coded:
                largest = jnp.full((half, CODE_ROWS, wide), jnp.max(jnp.abs(total)))
                exponent = jnp.floor(jnp.log2(CODE_TOP / jnp.maximum(largest, CODE_LEAST)))
                send_ref[:, :rows] = total * jnp.exp2(exponent[:, :1])
                send_ref[:, rows:] = exponent
            else:
                send_ref[...] = total.astype(send_ref.dtype)

        send, hold = self.call(
            body,
            [
                jax.ShapeDtypeStruct((half, rows + CODE_ROWS * coded, wide), jnp.float32 if coded else dtype),
                jax.ShapeDtypeStruct((half, rows, wide), jnp.float32),
            ],
            [received, kept],
            [VMEM] * 2,
        )
        return send.astype(dtype), hold

    def finish(self, received, kept):
        parts = len(kept)

        def body(*refs):
            for part in range(parts):
                refs[2 * parts + part][...] = refs[parts + part][0] + refs[part][0].astype(jnp.float32)

        shape = jax.ShapeDtypeStruct(kept[0].shape[1:], jnp.float32)
        return self.call(body, [shape] * parts, [*received, *kept], [VMEM] * (2 * parts))

    def finish_grads(self, scalars, received, kept):
        tokens, wide = kept[0].shape[1:]

        def body(scalars_ref, *refs):
            positions = lax.broadcasted_iota(jnp.int32, (tokens, wide), 0)
            valid = positions < scalars_ref[0]

            def grad(core):
                total = refs[2 + core][0] + decode(refs[core], tokens)[0]
                total = jnp.where(valid, total, jnp.zeros_like(total))
                return total.T.astype(jnp.bfloat16)

            mine_ref, other_ref = refs[4:]

            @pl.when(scalars_ref[1] == 0)
            def _():
                mine_ref[...] = grad(0)
                other_ref[...] = grad(1)

            @pl.when(scalars_ref[1] != 0)
            def _():
                mine_ref[...] = grad(1)
                other_ref[...] = grad(0)

        shape = jax.ShapeDtypeStruct((wide, tokens), jnp.bfloat16)
        return self.call(body, [shape] * 2, [scalars, *received, *kept], [SMEM] + [VMEM] * 4)

    def pair(self, mine, other):
        def body(mine_ref, other_ref, out_ref):
            out_ref[0, 0] = mine_ref[...]
            out_ref[0, 1] = other_ref[...]

        shape = jax.ShapeDtypeStruct((1, 2) + mine.shape, mine.dtype)
        return self.call(body, [shape], [mine, other], [VMEM] * 2)[0]

    def join(self, held, received):
        count = held.shape[0]

        def body(held_ref, received_ref, out_ref):
            out_ref[:count] = held_ref[...]
            out_ref[count:] = received_ref[...]

        shape = jax.ShapeDtypeStruct((2 * count,) + held.shape[1:], held.dtype)
        return self.call(body, [shape], [held, received], [VMEM] * 2)[0]

    def relay(self, x):
        def body(out_ref):
            out_ref[...] = jnp.zeros_like(out_ref)

        return self.call(body, [jax.ShapeDtypeStruct((8, LANES), jnp.float32)], [], [], carry=[x])[1]

    def moments(self, place, grads, acts, out_shape):
        rows, tokens = grads[0].shape[2:]
        count = sum(x.shape[0] for x in grads)
        blocks = len(acts)
        flat_acts = [x for block in acts for chunk in block for x in chunk]
        scale = 1.0 / SEQ_LEN**0.5

        def body(place_ref, *refs):
            grad_refs = refs[: len(grads)]
            act_refs = refs[len(grads) : len(grads) + len(flat_acts)]
            out_ref, result_ref, sems = refs[-3:]
            total = None
            for seq in range(SEQS):
                own = iter(act_refs[seq::SEQS])
                columns = [[next(own)[...] for _ in range(len(acts[block]))] for block in range(blocks)]
                act = jnp.concatenate([jnp.concatenate(column, axis=0) for column in columns], axis=1)
                high = act.astype(jnp.bfloat16)
                low = (act - high.astype(jnp.float32)).astype(jnp.bfloat16)
                grad = jnp.concatenate([ref[:, seq].reshape(-1, tokens) for ref in grad_refs], axis=0)
                rotated = jnp.dot(grad, high, preferred_element_type=jnp.float32)
                rotated = rotated + jnp.dot(grad, low, preferred_element_type=jnp.float32)
                rotated = rotated * scale
                squared = rotated * rotated
                total = squared if total is None else total + squared
            result_ref[...] = total / SEQS
            copies = []
            for at in range(count):
                start = pl.multiple_of(place_ref[at] * rows, rows)
                copies.append(
                    pltpu.make_async_copy(
                        result_ref.at[pl.ds(at * rows, rows)], out_ref.at[pl.ds(start, rows)], sems.at[at]
                    )
                )
                copies[-1].start()
            for copy in copies:
                copy.wait()

        inputs = [place, *grads, *flat_acts]
        specs = [SMEM] + [VMEM] * (len(inputs) - 1)
        return self.call(
            body,
            [out_shape],
            inputs,
            specs,
            out_specs=[ANY],
            scratch=[
                pltpu.VMEM((count * rows, out_shape.shape[1]), jnp.float32),
                pltpu.SemaphoreType.DMA((count,)),
            ],
            limit=24 * MIB,
        )[0]


def rotate_narrow(order, x, basis, width, start, slices, dtype):
    columns = basis[:, start * width : (start + slices) * width]
    rotated = jnp.dot(x, columns, preferred_element_type=jnp.float32)
    rotated = rotated.reshape(x.shape[0], slices, width).transpose(1, 0, 2)
    return [jnp.take(rotated, order, axis=0).astype(dtype)]


def halving_order(n, bits):
    return [sum((1 - ((at >> (bits - 1 - bit)) & 1)) << bit for bit in range(bits)) for at in range(n)]


def swap(x, n, bit):
    return lax.ppermute(x, "inp", [(index, index ^ (1 << bit)) for index in range(n)])


def swap_cores(x):
    return lax.ppermute(x, "out", [(0, 1), (1, 0)])


def on_device(acts, grads, basis_a, basis_g, lengths, *, n):
    bits = n.bit_length() - 1
    me = lax.axis_index("inp")
    core = lax.axis_index("out")
    scalars = jnp.stack([lengths[0], core]).astype(jnp.int32)
    x_a, x_g = acts[0], grads[0]
    width_a = basis_a.shape[1] // n
    width_g = basis_g.shape[1] // n // 2
    wide = min(WIDTH, width_a)
    blocks = width_a // wide
    chain = Chain()

    grad_keys = [("g", 0), ("g", 1)]
    act_keys = [("a", block, chunk) for block in range(blocks) for chunk in range(TOKEN_CHUNKS)]
    order = jnp.array(halving_order(n, bits), jnp.int32) ^ me
    orders = (order[: n // 2], order[n // 2 :])
    kept, received, finished, gathered = {}, {}, {}, {}
    def keep_or_send(key, x, part):
        if part == 0:
            received[key] = swap(x, n, 0)
        else:
            kept[key] = x

    def rotate_grads(half, part):
        key = ("g", half)
        order = orders[part]
        dtype = (jnp.bfloat16, jnp.float32)[part]
        if width_g % LANES == 0:
            (x,) = chain.rotate(order, x_g, basis_g, width_g, half * n, 1, order.shape[0], 1, dtype, 60 * MIB)
        else:
            (x,) = rotate_narrow(order, x_g, basis_g, width_g, half * n, n, dtype)
        keep_or_send(key, x, part)

    def rotate_acts(block, part):
        order = orders[part]
        dtype = (jnp.bfloat16, jnp.float32)[part]
        outs = chain.rotate(order, x_a, basis_a, wide, block, blocks, 2, TOKEN_CHUNKS, dtype)
        for chunk, x in enumerate(outs):
            keep_or_send(("a", block, chunk), x, part)

    def advance(key, step):
        wider = jnp.float16 if key[0] == "g" else jnp.float32
        dtype = jnp.bfloat16 if step + 1 < ROUNDED_STEPS[key[0]] else wider
        send, kept[key] = chain.combine(received[key], kept[key], dtype)
        arrived = swap(send, n, step + 1)
        received[key] = arrived.astype(jnp.float32) if dtype == jnp.float16 else arrived
        if key in EXPECTED and step + 2 == bits:
            chain.expect(received[key], EXPECTED[key])

    def finish_acts(block):
        keys = [("a", block, chunk) for chunk in range(TOKEN_CHUNKS)]
        own = chain.finish([received[key] for key in keys], [kept[key] for key in keys])
        finished[block] = [(x, swap_cores(x)) for x in own]

    def finish_grads():
        mine, other = chain.finish_grads(
            scalars, [received[key] for key in grad_keys], [kept[key] for key in grad_keys]
        )
        gathered["mine"], gathered["other"] = mine, swap_cores(other)

    def pair_grads():
        gathered["held"] = chain.pair(gathered["mine"], gathered["other"])
        gathered["order"] = [0]
        gathered["in"] = swap(gathered["held"], n, bits - 1)

    def join_grads(bit):
        gathered["held"] = chain.join(gathered["held"], gathered["in"])
        gathered["order"] = gathered["order"] + [at ^ (1 << bit) for at in gathered["order"]]
        gathered["in"] = swap(gathered["held"], n, bit - 1)
        if bit == 2:
            gathered["side"] = chain.expect(swap(gathered["held"], n, 0), SIDE_WAIT)

    def relay_grads():
        gathered["in"] = chain.relay(gathered["in"])
        gathered["across"] = chain.expect(swap(gathered["in"], n, 0), ACROSS_WAIT)

    tasks = [
        (0.0, rotate_grads, (0, 0)),
        (1.0, rotate_grads, (1, 0)),
        (2.0, rotate_grads, (0, 1)),
        (3.0, rotate_grads, (1, 1)),
    ]
    for block in range(blocks):
        tasks.append((SEND_AT[block], rotate_acts, (block, 0)))
        tasks.append((KEEP_AT[block], rotate_acts, (block, 1)))
    for key, times in zip(grad_keys + act_keys, STEPS_AT):
        for step in range(bits - 1):
            tasks.append((times[min(step, 1)] + 8.0 * max(step - 1, 0), advance, (key, step)))
    for block in range(blocks):
        tasks.append((FINISH_AT[block] + 8.0 * (bits - 3), finish_acts, (block,)))
    clock = GRADS_AT + 8.0 * (bits - 3)
    tasks.append((clock, finish_grads, ()))
    clock += 1.0
    tasks.append((clock, pair_grads, ()))
    for bit in range(bits - 1, 1, -1):
        clock += JOIN_WAIT
        tasks.append((clock, join_grads, (bit,)))
    tasks.append((clock + RELAY_WAIT, relay_grads, ()))
    for chain.clock, task, arguments in sorted(tasks, key=lambda task: task[0]):
        task(*arguments)

    low = gathered["order"]
    offsets = low + [at ^ 2 for at in low] + [at ^ 1 for at in low] + [at ^ 3 for at in low]
    place = jnp.array(offsets, jnp.int32) ^ me
    act_blocks = [finished[block] for block in range(blocks)]
    out_shape = jax.ShapeDtypeStruct((n * width_g, width_a), jnp.float32)
    grads = [gathered[name] for name in ("held", "in", "side", "across")]
    return chain.moments(place, grads, act_blocks, out_shape)


def solution(mesh):
    in_specs = (
        P(("group", "out"), None, "inp"),
        P(("group", "out"), None, "inp"),
        P(("group", "inp"), None),
        P(("group", "inp"), None),
        P(("group", "out")),
    )
    out_specs = P(("group", "out"), "inp")
    return jax.shard_map(
        functools.partial(on_device, n=mesh.shape["inp"]),
        mesh=mesh,
        in_specs=in_specs,
        out_specs=out_specs,
        check_vma=False,
    )
```

```python
import functools

import jax
import jax.numpy as jnp
from jax import lax
from jax.experimental import pallas as pl
from jax.experimental.pallas import tpu as pltpu
from jax.sharding import PartitionSpec as P

SEQ_LEN = 512
SEQS = 2
TOKEN_CHUNKS = 2
LANES = 128
WIDTH = 256
ROUNDED_STEPS = {"g": 2, "a": 3}
ANY = pl.BlockSpec(memory_space=pl.ANY)
CODE_ROWS = 16
CODE_TOP = 2.0**15
CODE_LEAST = 2.0**-100
VMEM = pl.BlockSpec(memory_space=pltpu.VMEM)
SMEM = pl.BlockSpec(memory_space=pltpu.SMEM)
MIB = 2**20
LIGHT = pl.CostEstimate(flops=0, bytes_accessed=2**17, transcendentals=0)


SEND_AT = (9.0, 21.9)
KEEP_AT = (32.5, 55.3)
STEPS_AT = ((21.7, 26.6), (30.0, 39.0), (42.0, 48.5), (52.0, 60.0), (61.0, 77.0), (72.3, 79.4))
FINISH_AT = (97.5, 100.0)
SQUARE_AT = (101.1, 200.0)
GRADS_AT = 45.9
JOIN_WAIT = 9.5
RELAY_WAIT = 20.1
SIDE_WAIT = 24.0
ACROSS_WAIT = 100.0
EXPECTED = {("g", 0): 9.5, ("a", 0, 0): 15.4, ("a", 0, 1): 24.5, ("a", 1, 0): 8.5, ("a", 1, 1): 23.2}


def decode(ref, rows):
    arrived = ref[...].astype(jnp.float32)
    if arrived.shape[1] == rows:
        return arrived
    return arrived[:, :rows] * jnp.exp2(-arrived[:, rows : rows + 1])


class Chain:
    def __init__(self):
        self.last = []
        self.clock = 0.0
        self.expected = []

    def expect(self, array, wait):
        self.expected.append((self.clock + wait, array))
        return array

    def waited_for(self):
        arrived = [array for due, array in self.expected if due <= self.clock]
        self.expected = [(due, array) for due, array in self.expected if due > self.clock]
        return self.last + arrived

    def call(self, body, out_shape, inputs, specs, out_specs=None, scratch=(), limit=8 * MIB, aliases=None, carry=()):
        unread = self.waited_for()
        deps = len(unread)

        carried = len(carry)
        aliases = dict(aliases or {})
        for at in range(carried):
            aliases[len(inputs) + deps + at] = len(out_shape) + at

        def kernel(*refs):
            rest = refs[len(inputs) + deps + carried :]
            body(*refs[: len(inputs)], *rest[: len(out_shape)], *rest[len(out_shape) + carried :])

        outs = pl.pallas_call(
            kernel,
            out_shape=list(out_shape) + [jax.ShapeDtypeStruct(x.shape, x.dtype) for x in carry],
            in_specs=list(specs) + [ANY] * (deps + carried),
            out_specs=(out_specs or [VMEM] * len(out_shape)) + [ANY] * carried,
            scratch_shapes=scratch,
            input_output_aliases=aliases,
            compiler_params=pltpu.CompilerParams(vmem_limit_bytes=limit),
            cost_estimate=LIGHT,
        )(*inputs, *unread, *carry)
        self.last = [outs[0]]
        return outs

    def rotate(self, order, part, x, basis, width, start, stride, per_step, chunks, dtype):
        tokens, features = x.shape
        count = order.shape[0] // 2
        first = part * count
        rows = tokens // chunks
        unread = self.waited_for()
        deps = len(unread)

        def kernel(order_ref, x_ref, *refs):
            del order_ref
            columns = jnp.concatenate([ref[...] for ref in refs[:per_step]], axis=1)
            rotated = jnp.dot(x_ref[...], columns, preferred_element_type=jnp.float32)
            for at in range(per_step):
                for chunk, ref in enumerate(refs[per_step + deps :]):
                    ref[at] = rotated[
                        chunk * rows : (chunk + 1) * rows, at * width : (at + 1) * width
                    ].astype(ref.dtype)

        def column_spec(at):
            return pl.BlockSpec(
                (features, width), lambda step, order: (0, order[first + step * per_step + at] * stride + start)
            )

        outs = pl.pallas_call(
            kernel,
            grid_spec=pltpu.PrefetchScalarGridSpec(
                num_scalar_prefetch=1,
                grid=(count // per_step,),
                in_specs=[VMEM]
                + [column_spec(at) for at in range(per_step)]
                + [ANY] * deps,
                out_specs=[pl.BlockSpec((per_step, rows, width), lambda step, order: (step, 0, 0))] * chunks,
            ),
            out_shape=[jax.ShapeDtypeStruct((count, rows, width), dtype)] * chunks,
            compiler_params=pltpu.CompilerParams(vmem_limit_bytes=24 * MIB),
            cost_estimate=LIGHT,
        )(order, x, *[basis] * per_step, *unread)
        self.last = [outs[0]]
        return outs

    def combine(self, received, kept, dtype):
        count, rows, wide = kept.shape
        half = count // 2
        coded = dtype == jnp.float16

        def body(received_ref, kept_ref, send_ref, hold_ref):
            arrived = decode(received_ref, rows)
            total = kept_ref[:half] + arrived[:half]
            hold_ref[...] = kept_ref[half:] + arrived[half:]
            if coded:
                largest = jnp.full((half, CODE_ROWS, wide), jnp.max(jnp.abs(total)))
                exponent = jnp.floor(jnp.log2(CODE_TOP / jnp.maximum(largest, CODE_LEAST)))
                send_ref[:, :rows] = total * jnp.exp2(exponent[:, :1])
                send_ref[:, rows:] = exponent
            else:
                send_ref[...] = total.astype(send_ref.dtype)

        send, hold = self.call(
            body,
            [
                jax.ShapeDtypeStruct((half, rows + CODE_ROWS * coded, wide), jnp.float32 if coded else dtype),
                jax.ShapeDtypeStruct((half, rows, wide), jnp.float32),
            ],
            [received, kept],
            [VMEM] * 2,
        )
        return send.astype(dtype), hold

    def finish(self, received, kept):
        parts = len(kept)

        def body(*refs):
            for part in range(parts):
                refs[2 * parts + part][...] = refs[parts + part][0] + refs[part][0].astype(jnp.float32)

        shape = jax.ShapeDtypeStruct(kept[0].shape[1:], jnp.float32)
        return self.call(body, [shape] * parts, [*received, *kept], [VMEM] * (2 * parts))

    def finish_grads(self, scalars, received, kept):
        tokens, wide = kept[0].shape[1:]

        def body(scalars_ref, *refs):
            positions = lax.broadcasted_iota(jnp.int32, (tokens, wide), 0)
            valid = positions < scalars_ref[0]

            def grad(core):
                total = refs[2 + core][0] + decode(refs[core], tokens)[0]
                total = jnp.where(valid, total, jnp.zeros_like(total))
                return total.T.astype(jnp.bfloat16)

            mine_ref, other_ref = refs[4:]

            @pl.when(scalars_ref[1] == 0)
            def _():
                mine_ref[...] = grad(0)
                other_ref[...] = grad(1)

            @pl.when(scalars_ref[1] != 0)
            def _():
                mine_ref[...] = grad(1)
                other_ref[...] = grad(0)

        shape = jax.ShapeDtypeStruct((wide, tokens), jnp.bfloat16)
        return self.call(body, [shape] * 2, [scalars, *received, *kept], [SMEM] + [VMEM] * 4)

    def pair(self, mine, other):
        def body(mine_ref, other_ref, out_ref):
            out_ref[0, 0] = mine_ref[...]
            out_ref[0, 1] = other_ref[...]

        shape = jax.ShapeDtypeStruct((1, 2) + mine.shape, mine.dtype)
        return self.call(body, [shape], [mine, other], [VMEM] * 2)[0]

    def join(self, held, received):
        count = held.shape[0]

        def body(held_ref, received_ref, out_ref):
            out_ref[:count] = held_ref[...]
            out_ref[count:] = received_ref[...]

        shape = jax.ShapeDtypeStruct((2 * count,) + held.shape[1:], held.dtype)
        return self.call(body, [shape], [held, received], [VMEM] * 2)[0]

    def relay(self, x):
        def body(out_ref):
            out_ref[...] = jnp.zeros_like(out_ref)

        return self.call(body, [jax.ShapeDtypeStruct((8, LANES), jnp.float32)], [], [], carry=[x])[1]

    def moments(self, place, grads, acts, block, out_shape, earlier=None):
        rows, tokens = grads[0].shape[2:]
        count = sum(x.shape[0] for x in grads)
        flat_acts = [x for chunk in acts for x in chunk]
        wide = flat_acts[0].shape[1]
        scale = 1.0 / SEQ_LEN**0.5

        def body(place_ref, *refs):
            grad_refs = refs[: len(grads)]
            act_refs = refs[len(grads) : len(grads) + len(flat_acts)]
            token_ref, out_ref, result_ref, sems = refs[-4:]
            token_ref[...] = jnp.zeros_like(token_ref)
            total = None
            for seq in range(SEQS):
                act = jnp.concatenate([ref[...] for ref in act_refs[seq::SEQS]], axis=0)
                high = act.astype(jnp.bfloat16)
                low = (act - high.astype(jnp.float32)).astype(jnp.bfloat16)
                grad = jnp.concatenate([ref[:, seq].reshape(-1, tokens) for ref in grad_refs], axis=0)
                rotated = jnp.dot(grad, high, preferred_element_type=jnp.float32)
                rotated = rotated + jnp.dot(grad, low, preferred_element_type=jnp.float32)
                rotated = rotated * scale
                squared = rotated * rotated
                total = squared if total is None else total + squared
            result_ref[...] = total / SEQS
            copies = []
            for at in range(count):
                start = pl.multiple_of(place_ref[at] * rows, rows)
                target = out_ref.at[pl.ds(start, rows), pl.ds(block * wide, wide)]
                copies.append(
                    pltpu.make_async_copy(result_ref.at[pl.ds(at * rows, rows)], target, sems.at[at])
                )
                copies[-1].start()
            for copy in copies:
                copy.wait()

        inputs = [place, *grads, *flat_acts]
        specs = [SMEM] + [VMEM] * (len(inputs) - 1)
        aliases = {}
        if earlier is not None:
            aliases = {len(inputs): 1}
            inputs.append(earlier)
            specs.append(ANY)
        return self.call(
            body,
            [jax.ShapeDtypeStruct((8, LANES), jnp.float32), out_shape],
            inputs,
            specs,
            out_specs=[VMEM, ANY],
            scratch=[pltpu.VMEM((count * rows, wide), jnp.float32), pltpu.SemaphoreType.DMA((count,))],
            limit=16 * MIB,
            aliases=aliases,
        )[1]


def rotate_narrow(order, x, basis, width, start, slices, dtype):
    columns = basis[:, start * width : (start + slices) * width]
    rotated = jnp.dot(x, columns, preferred_element_type=jnp.float32)
    rotated = rotated.reshape(x.shape[0], slices, width).transpose(1, 0, 2)
    return [jnp.take(rotated, order, axis=0).astype(dtype)]


def halving_order(n, bits):
    return [sum((1 - ((at >> (bits - 1 - bit)) & 1)) << bit for bit in range(bits)) for at in range(n)]


def swap(x, n, bit):
    return lax.ppermute(x, "inp", [(index, index ^ (1 << bit)) for index in range(n)])


def swap_cores(x):
    return lax.ppermute(x, "out", [(0, 1), (1, 0)])


def on_device(acts, grads, basis_a, basis_g, lengths, *, n):
    bits = n.bit_length() - 1
    me = lax.axis_index("inp")
    core = lax.axis_index("out")
    scalars = jnp.stack([lengths[0], core]).astype(jnp.int32)
    x_a, x_g = acts[0], grads[0]
    width_a = basis_a.shape[1] // n
    width_g = basis_g.shape[1] // n // 2
    wide = min(WIDTH, width_a)
    blocks = width_a // wide
    chain = Chain()

    grad_keys = [("g", 0), ("g", 1)]
    act_keys = [("a", block, chunk) for block in range(blocks) for chunk in range(TOKEN_CHUNKS)]
    order = jnp.array(halving_order(n, bits), jnp.int32) ^ me
    kept, received, finished, gathered = {}, {}, {}, {}
    def keep_or_send(key, x, part):
        if part == 0:
            received[key] = swap(x, n, 0)
        else:
            kept[key] = x

    def rotate_grads(half, part):
        key = ("g", half)
        dtype = (jnp.bfloat16, jnp.float32)[part]
        if width_g % LANES == 0:
            (x,) = chain.rotate(order, part, x_g, basis_g, width_g, half * n, 1, n // 2, 1, dtype)
        else:
            (x,) = rotate_narrow(order[part * n // 2 : (part + 1) * n // 2], x_g, basis_g, width_g, half * n, n, dtype)
        keep_or_send(key, x, part)

    def rotate_acts(block, part):
        dtype = (jnp.bfloat16, jnp.float32)[part]
        outs = chain.rotate(order, part, x_a, basis_a, wide, block, blocks, 2, TOKEN_CHUNKS, dtype)
        for chunk, x in enumerate(outs):
            keep_or_send(("a", block, chunk), x, part)

    def advance(key, step):
        wider = jnp.float16 if key[0] == "g" else jnp.float32
        dtype = jnp.bfloat16 if step + 1 < ROUNDED_STEPS[key[0]] else wider
        send, kept[key] = chain.combine(received[key], kept[key], dtype)
        arrived = swap(send, n, step + 1)
        received[key] = arrived.astype(jnp.float32) if dtype == jnp.float16 else arrived
        if key in EXPECTED and step + 2 == bits:
            chain.expect(received[key], EXPECTED[key])

    def finish_acts(block):
        keys = [("a", block, chunk) for chunk in range(TOKEN_CHUNKS)]
        own = chain.finish([received[key] for key in keys], [kept[key] for key in keys])
        finished[block] = [(x, swap_cores(x)) for x in own]

    def finish_grads():
        mine, other = chain.finish_grads(
            scalars, [received[key] for key in grad_keys], [kept[key] for key in grad_keys]
        )
        gathered["mine"], gathered["other"] = mine, swap_cores(other)

    def pair_grads():
        gathered["held"] = chain.pair(gathered["mine"], gathered["other"])
        gathered["order"] = [0]
        gathered["in"] = swap(gathered["held"], n, bits - 1)

    def join_grads(bit):
        gathered["held"] = chain.join(gathered["held"], gathered["in"])
        gathered["order"] = gathered["order"] + [at ^ (1 << bit) for at in gathered["order"]]
        gathered["in"] = swap(gathered["held"], n, bit - 1)
        if bit == 2:
            gathered["side"] = chain.expect(swap(gathered["held"], n, 0), SIDE_WAIT)

    def relay_grads():
        gathered["in"] = chain.relay(gathered["in"])
        gathered["across"] = chain.expect(swap(gathered["in"], n, 0), ACROSS_WAIT)

    tasks = [
        (0.0, rotate_grads, (0, 0)),
        (1.0, rotate_grads, (1, 0)),
        (2.0, rotate_grads, (0, 1)),
        (3.0, rotate_grads, (1, 1)),
    ]
    for block in range(blocks):
        tasks.append((SEND_AT[block], rotate_acts, (block, 0)))
        tasks.append((KEEP_AT[block], rotate_acts, (block, 1)))
    for key, times in zip(grad_keys + act_keys, STEPS_AT):
        for step in range(bits - 1):
            tasks.append((times[min(step, 1)] + 8.0 * max(step - 1, 0), advance, (key, step)))
    for block in range(blocks):
        tasks.append((FINISH_AT[block] + 8.0 * (bits - 3), finish_acts, (block,)))
    clock = GRADS_AT + 8.0 * (bits - 3)
    tasks.append((clock, finish_grads, ()))
    clock += 1.0
    tasks.append((clock, pair_grads, ()))
    for bit in range(bits - 1, 1, -1):
        clock += JOIN_WAIT
        tasks.append((clock, join_grads, (bit,)))
    tasks.append((clock + RELAY_WAIT, relay_grads, ()))
    out_shape = jax.ShapeDtypeStruct((n * width_g, width_a), jnp.float32)
    result = []

    def square(block):
        low = gathered["order"]
        offsets = low + [at ^ 2 for at in low] + [at ^ 1 for at in low] + [at ^ 3 for at in low]
        place = jnp.array(offsets, jnp.int32) ^ me
        grads = [gathered[name] for name in ("held", "in", "side", "across")]
        earlier = result[-1] if result else None
        result.append(chain.moments(place, grads, finished[block], block, out_shape, earlier))

    for block in range(blocks):
        tasks.append((SQUARE_AT[block] + 8.0 * (bits - 3), square, (block,)))
    for chain.clock, task, arguments in sorted(tasks, key=lambda task: task[0]):
        task(*arguments)
    return result[-1]


def solution(mesh):
    in_specs = (
        P(("group", "out"), None, "inp"),
        P(("group", "out"), None, "inp"),
        P(("group", "inp"), None),
        P(("group", "inp"), None),
        P(("group", "out")),
    )
    out_specs = P(("group", "out"), "inp")
    return jax.shard_map(
        functools.partial(on_device, n=mesh.shape["inp"]),
        mesh=mesh,
        in_specs=in_specs,
        out_specs=out_specs,
        check_vma=False,
    )
```

```python
import functools

import jax
import jax.numpy as jnp
from jax import lax
from jax.experimental import pallas as pl
from jax.experimental.pallas import tpu as pltpu
from jax.sharding import PartitionSpec as P

SEQ_LEN = 512
SEQS = 2
TOKEN_CHUNKS = 2
LANES = 128
WIDTH = 256
ROUNDED_STEPS = {"g": 2, "a": 3}
ANY = pl.BlockSpec(memory_space=pl.ANY)
CODE_ROWS = 16
CODE_TOP = 2.0**15
CODE_LEAST = 2.0**-100
VMEM = pl.BlockSpec(memory_space=pltpu.VMEM)
SMEM = pl.BlockSpec(memory_space=pltpu.SMEM)
MIB = 2**20
LIGHT = pl.CostEstimate(flops=0, bytes_accessed=2**17, transcendentals=0)


SEND_AT = (9.0, 21.9)
KEEP_AT = (32.5, 50.1)
STEPS_AT = ((21.7, 26.6), (30.0, 38.7), (42.0, 48.5), (52.0, 60.0), (55.6, 77.0), (72.3, 79.4))
FINISH_AT = (97.5, 100.0)
SQUARE_AT = (101.1, 200.0)
GRADS_AT = 44.0
JOIN_WAIT = 10.6
RELAY_WAIT = 20.1
NEAR_WAIT = 14.0
SIDE_WAIT = 29.2
ACROSS_WAIT = 100.0
EXPECTED = {("g", 0): 9.5, ("a", 0, 0): 15.4, ("a", 0, 1): 24.5, ("a", 1, 0): 8.5, ("a", 1, 1): 23.2}


def decode(ref, rows):
    arrived = ref[...].astype(jnp.float32)
    if arrived.shape[1] == rows:
        return arrived
    return arrived[:, :rows] * jnp.exp2(-arrived[:, rows : rows + 1])


class Chain:
    def __init__(self):
        self.last = []
        self.clock = 0.0
        self.expected = []

    def expect(self, array, wait):
        self.expected.append((self.clock + wait, array))
        return array

    def waited_for(self):
        arrived = [array for due, array in self.expected if due <= self.clock]
        self.expected = [(due, array) for due, array in self.expected if due > self.clock]
        return self.last + arrived

    def call(self, body, out_shape, inputs, specs, out_specs=None, scratch=(), limit=8 * MIB, aliases=None, carry=()):
        unread = self.waited_for()
        deps = len(unread)

        carried = len(carry)
        aliases = dict(aliases or {})
        for at in range(carried):
            aliases[len(inputs) + deps + at] = len(out_shape) + at

        def kernel(*refs):
            rest = refs[len(inputs) + deps + carried :]
            body(*refs[: len(inputs)], *rest[: len(out_shape)], *rest[len(out_shape) + carried :])

        outs = pl.pallas_call(
            kernel,
            out_shape=list(out_shape) + [jax.ShapeDtypeStruct(x.shape, x.dtype) for x in carry],
            in_specs=list(specs) + [ANY] * (deps + carried),
            out_specs=(out_specs or [VMEM] * len(out_shape)) + [ANY] * carried,
            scratch_shapes=scratch,
            input_output_aliases=aliases,
            compiler_params=pltpu.CompilerParams(vmem_limit_bytes=limit),
            cost_estimate=LIGHT,
        )(*inputs, *unread, *carry)
        self.last = [outs[0]]
        return outs

    def rotate(self, order, part, x, basis, width, start, stride, per_step, chunks, dtype):
        tokens, features = x.shape
        count = order.shape[0] // 2
        first = part * count
        rows = tokens // chunks
        unread = self.waited_for()
        deps = len(unread)

        def kernel(order_ref, x_ref, *refs):
            del order_ref
            columns = jnp.concatenate([ref[...] for ref in refs[:per_step]], axis=1)
            rotated = jnp.dot(x_ref[...], columns, preferred_element_type=jnp.float32)
            for at in range(per_step):
                for chunk, ref in enumerate(refs[per_step + deps :]):
                    ref[at] = rotated[
                        chunk * rows : (chunk + 1) * rows, at * width : (at + 1) * width
                    ].astype(ref.dtype)

        def column_spec(at):
            return pl.BlockSpec(
                (features, width), lambda step, order: (0, order[first + step * per_step + at] * stride + start)
            )

        outs = pl.pallas_call(
            kernel,
            grid_spec=pltpu.PrefetchScalarGridSpec(
                num_scalar_prefetch=1,
                grid=(count // per_step,),
                in_specs=[VMEM]
                + [column_spec(at) for at in range(per_step)]
                + [ANY] * deps,
                out_specs=[pl.BlockSpec((per_step, rows, width), lambda step, order: (step, 0, 0))] * chunks,
            ),
            out_shape=[jax.ShapeDtypeStruct((count, rows, width), dtype)] * chunks,
            compiler_params=pltpu.CompilerParams(vmem_limit_bytes=24 * MIB),
            cost_estimate=LIGHT,
        )(order, x, *[basis] * per_step, *unread)
        self.last = [outs[0]]
        return outs

    def combine(self, received, kept, dtype):
        count, rows, wide = kept.shape
        half = count // 2
        coded = dtype == jnp.float16

        def body(received_ref, kept_ref, send_ref, hold_ref):
            arrived = decode(received_ref, rows)
            total = kept_ref[:half] + arrived[:half]
            hold_ref[...] = kept_ref[half:] + arrived[half:]
            if coded:
                largest = jnp.full((half, CODE_ROWS, wide), jnp.max(jnp.abs(total)))
                exponent = jnp.floor(jnp.log2(CODE_TOP / jnp.maximum(largest, CODE_LEAST)))
                send_ref[:, :rows] = total * jnp.exp2(exponent[:, :1])
                send_ref[:, rows:] = exponent
            else:
                send_ref[...] = total.astype(send_ref.dtype)

        send, hold = self.call(
            body,
            [
                jax.ShapeDtypeStruct((half, rows + CODE_ROWS * coded, wide), jnp.float32 if coded else dtype),
                jax.ShapeDtypeStruct((half, rows, wide), jnp.float32),
            ],
            [received, kept],
            [VMEM] * 2,
        )
        return send.astype(dtype), hold

    def finish(self, received, kept):
        parts = len(kept)

        def body(*refs):
            for part in range(parts):
                refs[2 * parts + part][...] = refs[parts + part][0] + refs[part][0].astype(jnp.float32)

        shape = jax.ShapeDtypeStruct(kept[0].shape[1:], jnp.float32)
        return self.call(body, [shape] * parts, [*received, *kept], [VMEM] * (2 * parts))

    def finish_grads(self, scalars, received, kept):
        tokens, wide = kept[0].shape[1:]

        def body(scalars_ref, *refs):
            positions = lax.broadcasted_iota(jnp.int32, (tokens, wide), 0)
            valid = positions < scalars_ref[0]

            def grad(core):
                total = refs[2 + core][0] + decode(refs[core], tokens)[0]
                total = jnp.where(valid, total, jnp.zeros_like(total))
                return total.T.astype(jnp.bfloat16)

            mine_ref, other_ref = refs[4:]

            @pl.when(scalars_ref[1] == 0)
            def _():
                mine_ref[...] = grad(0)
                other_ref[...] = grad(1)

            @pl.when(scalars_ref[1] != 0)
            def _():
                mine_ref[...] = grad(1)
                other_ref[...] = grad(0)

        shape = jax.ShapeDtypeStruct((wide, tokens), jnp.bfloat16)
        return self.call(body, [shape] * 2, [scalars, *received, *kept], [SMEM] + [VMEM] * 4)

    def pair(self, mine, other):
        def body(mine_ref, other_ref, out_ref):
            out_ref[0, 0] = mine_ref[...]
            out_ref[0, 1] = other_ref[...]

        shape = jax.ShapeDtypeStruct((1, 2) + mine.shape, mine.dtype)
        return self.call(body, [shape], [mine, other], [VMEM] * 2)[0]

    def join(self, held, received):
        count = held.shape[0]

        def body(held_ref, received_ref, out_ref):
            out_ref[:count] = held_ref[...]
            out_ref[count:] = received_ref[...]

        shape = jax.ShapeDtypeStruct((2 * count,) + held.shape[1:], held.dtype)
        return self.call(body, [shape], [held, received], [VMEM] * 2)[0]

    def moments(self, place, grads, acts, block, out_shape, earlier=None):
        rows, tokens = grads[0].shape[2:]
        count = sum(x.shape[0] for x in grads)
        flat_acts = [x for chunk in acts for x in chunk]
        wide = flat_acts[0].shape[1]
        scale = 1.0 / SEQ_LEN**0.5

        def body(place_ref, *refs):
            grad_refs = refs[: len(grads)]
            act_refs = refs[len(grads) : len(grads) + len(flat_acts)]
            token_ref, out_ref, result_ref, sems = refs[-4:]
            token_ref[...] = jnp.zeros_like(token_ref)
            total = None
            for seq in range(SEQS):
                act = jnp.concatenate([ref[...] for ref in act_refs[seq::SEQS]], axis=0)
                high = act.astype(jnp.bfloat16)
                low = (act - high.astype(jnp.float32)).astype(jnp.bfloat16)
                grad = jnp.concatenate([ref[:, seq].reshape(-1, tokens) for ref in grad_refs], axis=0)
                rotated = jnp.dot(grad, high, preferred_element_type=jnp.float32)
                rotated = rotated + jnp.dot(grad, low, preferred_element_type=jnp.float32)
                rotated = rotated * scale
                squared = rotated * rotated
                total = squared if total is None else total + squared
            result_ref[...] = total / SEQS
            copies = []
            for at in range(count):
                start = pl.multiple_of(place_ref[at] * rows, rows)
                target = out_ref.at[pl.ds(start, rows), pl.ds(block * wide, wide)]
                copies.append(
                    pltpu.make_async_copy(result_ref.at[pl.ds(at * rows, rows)], target, sems.at[at])
                )
                copies[-1].start()
            for copy in copies:
                copy.wait()

        inputs = [place, *grads, *flat_acts]
        specs = [SMEM] + [VMEM] * (len(inputs) - 1)
        aliases = {}
        if earlier is not None:
            aliases = {len(inputs): 1}
            inputs.append(earlier)
            specs.append(ANY)
        return self.call(
            body,
            [jax.ShapeDtypeStruct((8, LANES), jnp.float32), out_shape],
            inputs,
            specs,
            out_specs=[VMEM, ANY],
            scratch=[pltpu.VMEM((count * rows, wide), jnp.float32), pltpu.SemaphoreType.DMA((count,))],
            limit=16 * MIB,
            aliases=aliases,
        )[1]


def rotate_narrow(order, x, basis, width, start, slices, dtype):
    columns = basis[:, start * width : (start + slices) * width]
    rotated = jnp.dot(x, columns, preferred_element_type=jnp.float32)
    rotated = rotated.reshape(x.shape[0], slices, width).transpose(1, 0, 2)
    return [jnp.take(rotated, order, axis=0).astype(dtype)]


def halving_order(n, bits):
    return [sum((1 - ((at >> (bits - 1 - bit)) & 1)) << bit for bit in range(bits)) for at in range(n)]


def swap(x, n, bit):
    return lax.ppermute(x, "inp", [(index, index ^ (1 << bit)) for index in range(n)])


def swap_cores(x):
    return lax.ppermute(x, "out", [(0, 1), (1, 0)])


def on_device(acts, grads, basis_a, basis_g, lengths, *, n):
    bits = n.bit_length() - 1
    me = lax.axis_index("inp")
    core = lax.axis_index("out")
    scalars = jnp.stack([lengths[0], core]).astype(jnp.int32)
    x_a, x_g = acts[0], grads[0]
    width_a = basis_a.shape[1] // n
    width_g = basis_g.shape[1] // n // 2
    wide = min(WIDTH, width_a)
    blocks = width_a // wide
    chain = Chain()

    grad_keys = [("g", 0), ("g", 1)]
    act_keys = [("a", block, chunk) for block in range(blocks) for chunk in range(TOKEN_CHUNKS)]
    order = jnp.array(halving_order(n, bits), jnp.int32) ^ me
    kept, received, finished, gathered, advanced = {}, {}, {}, {}, {}
    def keep_or_send(key, x, part):
        if part == 0:
            received[key] = swap(x, n, 0)
        else:
            kept[key] = x

    def rotate_grads(half, part):
        key = ("g", half)
        dtype = (jnp.bfloat16, jnp.float32)[part]
        if width_g % LANES == 0:
            (x,) = chain.rotate(order, part, x_g, basis_g, width_g, half * n, 1, n // 2, 1, dtype)
        else:
            (x,) = rotate_narrow(order[part * n // 2 : (part + 1) * n // 2], x_g, basis_g, width_g, half * n, n, dtype)
        keep_or_send(key, x, part)

    def rotate_acts(block, part):
        dtype = (jnp.bfloat16, jnp.float32)[part]
        outs = chain.rotate(order, part, x_a, basis_a, wide, block, blocks, 2, TOKEN_CHUNKS, dtype)
        for chunk, x in enumerate(outs):
            keep_or_send(("a", block, chunk), x, part)

    def advance(key, step):
        assert step == advanced.get(key, 0)
        advanced[key] = step + 1
        wider = jnp.float16 if key[0] == "g" else jnp.float32
        dtype = jnp.bfloat16 if step + 1 < ROUNDED_STEPS[key[0]] else wider
        send, kept[key] = chain.combine(received[key], kept[key], dtype)
        arrived = swap(send, n, step + 1)
        received[key] = arrived.astype(jnp.float32) if dtype == jnp.float16 else arrived
        if key in EXPECTED and step + 2 == bits:
            chain.expect(received[key], EXPECTED[key])

    def finish_acts(block):
        keys = [("a", block, chunk) for chunk in range(TOKEN_CHUNKS)]
        assert all(advanced[key] == bits - 1 for key in keys)
        own = chain.finish([received[key] for key in keys], [kept[key] for key in keys])
        finished[block] = [(x, swap_cores(x)) for x in own]

    def finish_grads():
        assert all(advanced[key] == bits - 1 for key in grad_keys)
        mine, other = chain.finish_grads(
            scalars, [received[key] for key in grad_keys], [kept[key] for key in grad_keys]
        )
        gathered["mine"], gathered["other"] = mine, swap_cores(other)

    def pair_grads():
        gathered["held"] = chain.pair(gathered["mine"], gathered["other"])
        gathered["order"] = [0]
        send_grads(bits - 1)

    def send_grads(bit):
        gathered["in"] = swap(gathered["held"], n, bit)
        if bit == 2:
            gathered["near"] = chain.expect(swap(gathered["held"], n, 1), NEAR_WAIT)

    def join_grads(bit):
        received = gathered["in"]
        if bit == 2:
            gathered["far"] = swap(received, n, 1)
        gathered["held"] = chain.join(gathered["held"], received)
        gathered["order"] = gathered["order"] + [at ^ (1 << bit) for at in gathered["order"]]
        if bit == 2:
            gathered["side"] = chain.expect(swap(gathered["held"], n, 0), SIDE_WAIT)
        else:
            send_grads(bit - 1)

    def relay_grads():
        gathered["in"] = chain.join(gathered["near"], gathered["far"])
        gathered["across"] = chain.expect(swap(gathered["in"], n, 0), ACROSS_WAIT)

    tasks = [
        (0.0, rotate_grads, (0, 0)),
        (1.0, rotate_grads, (1, 0)),
        (2.0, rotate_grads, (0, 1)),
        (3.0, rotate_grads, (1, 1)),
    ]
    for block in range(blocks):
        tasks.append((SEND_AT[block], rotate_acts, (block, 0)))
        tasks.append((KEEP_AT[block], rotate_acts, (block, 1)))
    for key, times in zip(grad_keys + act_keys, STEPS_AT):
        for step in range(bits - 1):
            tasks.append((times[min(step, 1)] + 8.0 * max(step - 1, 0), advance, (key, step)))
    for block in range(blocks):
        tasks.append((FINISH_AT[block] + 8.0 * (bits - 3), finish_acts, (block,)))
    clock = GRADS_AT + 8.0 * (bits - 3)
    tasks.append((clock, finish_grads, ()))
    clock += 1.0
    tasks.append((clock, pair_grads, ()))
    for bit in range(bits - 1, 1, -1):
        clock += JOIN_WAIT
        tasks.append((clock, join_grads, (bit,)))
    tasks.append((clock + RELAY_WAIT, relay_grads, ()))
    out_shape = jax.ShapeDtypeStruct((n * width_g, width_a), jnp.float32)
    result = []

    def square(block):
        low = gathered["order"]
        offsets = low + [at ^ 2 for at in low] + [at ^ 1 for at in low] + [at ^ 3 for at in low]
        place = jnp.array(offsets, jnp.int32) ^ me
        grads = [gathered[name] for name in ("held", "in", "side", "across")]
        assert "across" in gathered
        earlier = result[-1] if result else None
        result.append(chain.moments(place, grads, finished[block], block, out_shape, earlier))

    for block in range(blocks):
        tasks.append((SQUARE_AT[block] + 8.0 * (bits - 3), square, (block,)))
    for chain.clock, task, arguments in sorted(tasks, key=lambda task: task[0]):
        task(*arguments)
    return result[-1]


def solution(mesh):
    in_specs = (
        P(("group", "out"), None, "inp"),
        P(("group", "out"), None, "inp"),
        P(("group", "inp"), None),
        P(("group", "inp"), None),
        P(("group", "out")),
    )
    out_specs = P(("group", "out"), "inp")
    return jax.shard_map(
        functools.partial(on_device, n=mesh.shape["inp"]),
        mesh=mesh,
        in_specs=in_specs,
        out_specs=out_specs,
        check_vma=False,
    )
```

```python
import functools

import jax
import jax.numpy as jnp
from jax import lax
from jax.experimental import pallas as pl
from jax.experimental.pallas import tpu as pltpu
from jax.sharding import PartitionSpec as P

SEQ_LEN = 512
SEQS = 2
TOKEN_CHUNKS = 2
LANES = 128
WIDTH = 256
ROUNDED_STEPS = {"g": 2, "a": 3}
ANY = pl.BlockSpec(memory_space=pl.ANY)
CODE_ROWS = 16
CODE_TOP = 2.0**15
CODE_LEAST = 2.0**-100
VMEM = pl.BlockSpec(memory_space=pltpu.VMEM)
SMEM = pl.BlockSpec(memory_space=pltpu.SMEM)
MIB = 2**20
LIGHT = pl.CostEstimate(flops=0, bytes_accessed=2**17, transcendentals=0)


SEND_AT = (9.0, 21.9)
KEEP_AT = (32.5, 50.1)
STEPS_AT = ((21.7, 26.6), (30.0, 38.7), (42.0, 48.5), (52.0, 60.0), (55.4, 77.0), (72.3, 79.4))
FINISH_AT = (97.5, 100.0)
SQUARE_AT = (101.1, 200.0)
GRADS_AT = 44.0
JOIN_WAIT = 10.6
RELAY_WAIT = 20.1
NEAR_WAIT = 14.0
SIDE_WAIT = 100.0
ACROSS_WAIT = 100.0
EXPECTED = {("g", 0): 9.5, ("a", 0, 0): 15.4, ("a", 0, 1): 24.5, ("a", 1, 0): 8.5, ("a", 1, 1): 23.2}


def decode(ref, rows):
    arrived = ref[...].astype(jnp.float32)
    if arrived.shape[1] == rows:
        return arrived
    return arrived[:, :rows] * jnp.exp2(-arrived[:, rows : rows + 1])


class Chain:
    def __init__(self):
        self.last = []
        self.clock = 0.0
        self.expected = []

    def expect(self, array, wait):
        self.expected.append((self.clock + wait, array))
        return array

    def waited_for(self):
        arrived = [array for due, array in self.expected if due <= self.clock]
        self.expected = [(due, array) for due, array in self.expected if due > self.clock]
        return self.last + arrived

    def call(self, body, out_shape, inputs, specs, out_specs=None, scratch=(), limit=8 * MIB, aliases=None, carry=()):
        unread = self.waited_for()
        deps = len(unread)

        carried = len(carry)
        aliases = dict(aliases or {})
        for at in range(carried):
            aliases[len(inputs) + deps + at] = len(out_shape) + at

        def kernel(*refs):
            rest = refs[len(inputs) + deps + carried :]
            body(*refs[: len(inputs)], *rest[: len(out_shape)], *rest[len(out_shape) + carried :])

        outs = pl.pallas_call(
            kernel,
            out_shape=list(out_shape) + [jax.ShapeDtypeStruct(x.shape, x.dtype) for x in carry],
            in_specs=list(specs) + [ANY] * (deps + carried),
            out_specs=(out_specs or [VMEM] * len(out_shape)) + [ANY] * carried,
            scratch_shapes=scratch,
            input_output_aliases=aliases,
            compiler_params=pltpu.CompilerParams(vmem_limit_bytes=limit),
            cost_estimate=LIGHT,
        )(*inputs, *unread, *carry)
        self.last = [outs[0]]
        return outs

    def rotate(self, order, part, x, basis, width, start, stride, per_step, chunks, dtype):
        tokens, features = x.shape
        count = order.shape[0] // 2
        first = part * count
        rows = tokens // chunks
        unread = self.waited_for()
        deps = len(unread)

        def kernel(order_ref, x_ref, *refs):
            del order_ref
            columns = jnp.concatenate([ref[...] for ref in refs[:per_step]], axis=1)
            rotated = jnp.dot(x_ref[...], columns, preferred_element_type=jnp.float32)
            for at in range(per_step):
                for chunk, ref in enumerate(refs[per_step + deps :]):
                    ref[at] = rotated[
                        chunk * rows : (chunk + 1) * rows, at * width : (at + 1) * width
                    ].astype(ref.dtype)

        def column_spec(at):
            return pl.BlockSpec(
                (features, width), lambda step, order: (0, order[first + step * per_step + at] * stride + start)
            )

        outs = pl.pallas_call(
            kernel,
            grid_spec=pltpu.PrefetchScalarGridSpec(
                num_scalar_prefetch=1,
                grid=(count // per_step,),
                in_specs=[VMEM]
                + [column_spec(at) for at in range(per_step)]
                + [ANY] * deps,
                out_specs=[pl.BlockSpec((per_step, rows, width), lambda step, order: (step, 0, 0))] * chunks,
            ),
            out_shape=[jax.ShapeDtypeStruct((count, rows, width), dtype)] * chunks,
            compiler_params=pltpu.CompilerParams(vmem_limit_bytes=24 * MIB),
            cost_estimate=LIGHT,
        )(order, x, *[basis] * per_step, *unread)
        self.last = [outs[0]]
        return outs

    def combine(self, received, kept, dtype):
        count, rows, wide = kept.shape
        half = count // 2
        coded = dtype == jnp.float16

        def body(received_ref, kept_ref, send_ref, hold_ref):
            arrived = decode(received_ref, rows)
            total = kept_ref[:half] + arrived[:half]
            hold_ref[...] = kept_ref[half:] + arrived[half:]
            if coded:
                largest = jnp.full((half, CODE_ROWS, wide), jnp.max(jnp.abs(total)))
                exponent = jnp.floor(jnp.log2(CODE_TOP / jnp.maximum(largest, CODE_LEAST)))
                send_ref[:, :rows] = total * jnp.exp2(exponent[:, :1])
                send_ref[:, rows:] = exponent
            else:
                send_ref[...] = total.astype(send_ref.dtype)

        send, hold = self.call(
            body,
            [
                jax.ShapeDtypeStruct((half, rows + CODE_ROWS * coded, wide), jnp.float32 if coded else dtype),
                jax.ShapeDtypeStruct((half, rows, wide), jnp.float32),
            ],
            [received, kept],
            [VMEM] * 2,
        )
        return send.astype(dtype), hold

    def finish(self, received, kept):
        parts = len(kept)

        def body(*refs):
            for part in range(parts):
                refs[2 * parts + part][...] = refs[parts + part][0] + refs[part][0].astype(jnp.float32)

        shape = jax.ShapeDtypeStruct(kept[0].shape[1:], jnp.float32)
        return self.call(body, [shape] * parts, [*received, *kept], [VMEM] * (2 * parts))

    def finish_grads(self, scalars, received, kept):
        tokens, wide = kept[0].shape[1:]

        def body(scalars_ref, *refs):
            positions = lax.broadcasted_iota(jnp.int32, (tokens, wide), 0)
            valid = positions < scalars_ref[0]

            def grad(core):
                total = refs[2 + core][0] + decode(refs[core], tokens)[0]
                total = jnp.where(valid, total, jnp.zeros_like(total))
                return total.T.astype(jnp.bfloat16)

            mine_ref, other_ref = refs[4:]

            @pl.when(scalars_ref[1] == 0)
            def _():
                mine_ref[...] = grad(0)
                other_ref[...] = grad(1)

            @pl.when(scalars_ref[1] != 0)
            def _():
                mine_ref[...] = grad(1)
                other_ref[...] = grad(0)

        shape = jax.ShapeDtypeStruct((wide, tokens), jnp.bfloat16)
        return self.call(body, [shape] * 2, [scalars, *received, *kept], [SMEM] + [VMEM] * 4)

    def pair(self, mine, other):
        def body(mine_ref, other_ref, out_ref):
            out_ref[0, 0] = mine_ref[...]
            out_ref[0, 1] = other_ref[...]

        shape = jax.ShapeDtypeStruct((1, 2) + mine.shape, mine.dtype)
        return self.call(body, [shape], [mine, other], [VMEM] * 2)[0]

    def join(self, held, received):
        count = held.shape[0]

        def body(held_ref, received_ref, out_ref):
            out_ref[:count] = held_ref[...]
            out_ref[count:] = received_ref[...]

        shape = jax.ShapeDtypeStruct((2 * count,) + held.shape[1:], held.dtype)
        return self.call(body, [shape], [held, received], [VMEM] * 2)[0]

    def moments(self, place, grads, acts, block, out_shape, earlier=None):
        rows, tokens = grads[0].shape[2:]
        count = sum(x.shape[0] for x in grads)
        flat_acts = [x for chunk in acts for x in chunk]
        wide = flat_acts[0].shape[1]
        scale = 1.0 / SEQ_LEN**0.5

        def body(place_ref, *refs):
            grad_refs = refs[: len(grads)]
            act_refs = refs[len(grads) : len(grads) + len(flat_acts)]
            token_ref, out_ref, result_ref, sems = refs[-4:]
            token_ref[...] = jnp.zeros_like(token_ref)
            total = None
            for seq in range(SEQS):
                act = jnp.concatenate([ref[...] for ref in act_refs[seq::SEQS]], axis=0)
                high = act.astype(jnp.bfloat16)
                low = (act - high.astype(jnp.float32)).astype(jnp.bfloat16)
                grad = jnp.concatenate([ref[:, seq].reshape(-1, tokens) for ref in grad_refs], axis=0)
                rotated = jnp.dot(grad, high, preferred_element_type=jnp.float32)
                rotated = rotated + jnp.dot(grad, low, preferred_element_type=jnp.float32)
                rotated = rotated * scale
                squared = rotated * rotated
                total = squared if total is None else total + squared
            result_ref[...] = total / SEQS
            copies = []
            for at in range(count):
                start = pl.multiple_of(place_ref[at] * rows, rows)
                target = out_ref.at[pl.ds(start, rows), pl.ds(block * wide, wide)]
                copies.append(
                    pltpu.make_async_copy(result_ref.at[pl.ds(at * rows, rows)], target, sems.at[at])
                )
                copies[-1].start()
            for copy in copies:
                copy.wait()

        inputs = [place, *grads, *flat_acts]
        specs = [SMEM] + [VMEM] * (len(inputs) - 1)
        aliases = {}
        if earlier is not None:
            aliases = {len(inputs): 1}
            inputs.append(earlier)
            specs.append(ANY)
        return self.call(
            body,
            [jax.ShapeDtypeStruct((8, LANES), jnp.float32), out_shape],
            inputs,
            specs,
            out_specs=[VMEM, ANY],
            scratch=[pltpu.VMEM((count * rows, wide), jnp.float32), pltpu.SemaphoreType.DMA((count,))],
            limit=16 * MIB,
            aliases=aliases,
        )[1]


def rotate_narrow(order, x, basis, width, start, slices, dtype):
    columns = basis[:, start * width : (start + slices) * width]
    rotated = jnp.dot(x, columns, preferred_element_type=jnp.float32)
    rotated = rotated.reshape(x.shape[0], slices, width).transpose(1, 0, 2)
    return [jnp.take(rotated, order, axis=0).astype(dtype)]


def halving_order(n, bits):
    return [sum((1 - ((at >> (bits - 1 - bit)) & 1)) << bit for bit in range(bits)) for at in range(n)]


def swap(x, n, bit):
    return lax.ppermute(x, "inp", [(index, index ^ (1 << bit)) for index in range(n)])


def swap_cores(x):
    return lax.ppermute(x, "out", [(0, 1), (1, 0)])


def on_device(acts, grads, basis_a, basis_g, lengths, *, n):
    bits = n.bit_length() - 1
    me = lax.axis_index("inp")
    core = lax.axis_index("out")
    scalars = jnp.stack([lengths[0], core]).astype(jnp.int32)
    x_a, x_g = acts[0], grads[0]
    width_a = basis_a.shape[1] // n
    width_g = basis_g.shape[1] // n // 2
    wide = min(WIDTH, width_a)
    blocks = width_a // wide
    chain = Chain()

    grad_keys = [("g", 0), ("g", 1)]
    act_keys = [("a", block, chunk) for block in range(blocks) for chunk in range(TOKEN_CHUNKS)]
    order = jnp.array(halving_order(n, bits), jnp.int32) ^ me
    kept, received, finished, gathered, advanced = {}, {}, {}, {}, {}
    def keep_or_send(key, x, part):
        if part == 0:
            received[key] = swap(x, n, 0)
        else:
            kept[key] = x

    def rotate_grads(half, part):
        key = ("g", half)
        dtype = (jnp.bfloat16, jnp.float32)[part]
        if width_g % LANES == 0:
            (x,) = chain.rotate(order, part, x_g, basis_g, width_g, half * n, 1, n // 2, 1, dtype)
        else:
            (x,) = rotate_narrow(order[part * n // 2 : (part + 1) * n // 2], x_g, basis_g, width_g, half * n, n, dtype)
        keep_or_send(key, x, part)

    def rotate_acts(block, part):
        dtype = (jnp.bfloat16, jnp.float32)[part]
        outs = chain.rotate(order, part, x_a, basis_a, wide, block, blocks, 2, TOKEN_CHUNKS, dtype)
        for chunk, x in enumerate(outs):
            keep_or_send(("a", block, chunk), x, part)

    def advance(key, step):
        assert step == advanced.get(key, 0)
        advanced[key] = step + 1
        wider = jnp.float16 if key[0] == "g" else jnp.float32
        dtype = jnp.bfloat16 if step + 1 < ROUNDED_STEPS[key[0]] else wider
        send, kept[key] = chain.combine(received[key], kept[key], dtype)
        arrived = swap(send, n, step + 1)
        received[key] = arrived.astype(jnp.float32) if dtype == jnp.float16 else arrived
        if key in EXPECTED and step + 2 == bits:
            chain.expect(received[key], EXPECTED[key])

    def finish_acts(block):
        keys = [("a", block, chunk) for chunk in range(TOKEN_CHUNKS)]
        assert all(advanced[key] == bits - 1 for key in keys)
        own = chain.finish([received[key] for key in keys], [kept[key] for key in keys])
        finished[block] = [(x, swap_cores(x)) for x in own]

    def finish_grads():
        assert all(advanced[key] == bits - 1 for key in grad_keys)
        mine, other = chain.finish_grads(
            scalars, [received[key] for key in grad_keys], [kept[key] for key in grad_keys]
        )
        gathered["mine"], gathered["other"] = mine, swap_cores(other)

    def pair_grads():
        gathered["held"] = chain.pair(gathered["mine"], gathered["other"])
        gathered["order"] = [0]
        send_grads(bits - 1)

    def send_grads(bit):
        gathered["in"] = swap(gathered["held"], n, bit)
        if bit == 2:
            gathered["near"] = chain.expect(swap(gathered["held"], n, 1), NEAR_WAIT)

    def join_grads(bit):
        received = gathered["in"]
        if bit == 2:
            gathered["far"] = swap(received, n, 1)
        gathered["held"] = chain.join(gathered["held"], received)
        gathered["order"] = gathered["order"] + [at ^ (1 << bit) for at in gathered["order"]]
        if bit == 2:
            gathered["side"] = chain.expect(swap(gathered["held"], n, 0), SIDE_WAIT)
        else:
            send_grads(bit - 1)

    def relay_grads():
        gathered["in"] = chain.join(gathered["near"], gathered["far"])
        gathered["across"] = chain.expect(swap(gathered["in"], n, 0), ACROSS_WAIT)

    tasks = [
        (0.0, rotate_grads, (0, 0)),
        (1.0, rotate_grads, (1, 0)),
        (2.0, rotate_grads, (0, 1)),
        (3.0, rotate_grads, (1, 1)),
    ]
    for block in range(blocks):
        tasks.append((SEND_AT[block], rotate_acts, (block, 0)))
        tasks.append((KEEP_AT[block], rotate_acts, (block, 1)))
    for key, times in zip(grad_keys + act_keys, STEPS_AT):
        for step in range(bits - 1):
            tasks.append((times[min(step, 1)] + 8.0 * max(step - 1, 0), advance, (key, step)))
    for block in range(blocks):
        tasks.append((FINISH_AT[block] + 8.0 * (bits - 3), finish_acts, (block,)))
    clock = GRADS_AT + 8.0 * (bits - 3)
    tasks.append((clock, finish_grads, ()))
    clock += 1.0
    tasks.append((clock, pair_grads, ()))
    for bit in range(bits - 1, 1, -1):
        clock += JOIN_WAIT
        tasks.append((clock, join_grads, (bit,)))
    tasks.append((clock + RELAY_WAIT, relay_grads, ()))
    out_shape = jax.ShapeDtypeStruct((n * width_g, width_a), jnp.float32)
    result = []

    def square(block):
        low = gathered["order"]
        offsets = low + [at ^ 2 for at in low] + [at ^ 1 for at in low] + [at ^ 3 for at in low]
        place = jnp.array(offsets, jnp.int32) ^ me
        grads = [gathered[name] for name in ("held", "in", "side", "across")]
        assert "across" in gathered
        earlier = result[-1] if result else None
        result.append(chain.moments(place, grads, finished[block], block, out_shape, earlier))

    for block in range(blocks):
        tasks.append((SQUARE_AT[block] + 8.0 * (bits - 3), square, (block,)))
    for chain.clock, task, arguments in sorted(tasks, key=lambda task: task[0]):
        task(*arguments)
    return result[-1]


def solution(mesh):
    in_specs = (
        P(("group", "out"), None, "inp"),
        P(("group", "out"), None, "inp"),
        P(("group", "inp"), None),
        P(("group", "inp"), None),
        P(("group", "out")),
    )
    out_specs = P(("group", "out"), "inp")
    return jax.shard_map(
        functools.partial(on_device, n=mesh.shape["inp"]),
        mesh=mesh,
        in_specs=in_specs,
        out_specs=out_specs,
        check_vma=False,
    )
```
